256 devices in a mesh: freq: 16 (over y, x), node: 16 (over z, core).
Axes of the slice: x: 4, y: 4, z: 8, core: 2. Of those that a mesh axis runs over, the one named last changes fastest.
Arguments:
- harmonics: float32 [64, 2, 3, 32768], P('freq', None, None, 'node'), may hold values from -6 to 6
- forcing: float32 [64, 2, 3, 32768], P('freq', None, None, 'node'), may hold values from -6 to 6
- depths: float32 [32768], P('node'), may hold values from 1 to 8
- damping: float32 [32768], P('node'), may hold values from 0.2 to 2
- weights: float32 [4, 32768], P(None, 'node'), may hold values from 0.1 to 1
- couple_east: float32 [4, 32768], P(None, 'node'), may hold values from -0.3 to 0.3
- couple_north: float32 [4, 32768], P(None, 'node'), may hold values from -0.3 to 0.3
- connections: int32 [256, 4], P('node'), may hold values from 0 to 255, as said below
- counts: int32 [2, 64], replicated, may hold values from 1 to 5, as said below
- harmonic_of_slot: int32 [64], replicated, may hold values from 0 to 63, each once
Outputs:
- solution: float32 [64, 2, 3, 32768], P('freq', None, None, 'node')
- residual: float32 [64, 2, 3, 32768], P('freq', None, None, 'node')
The draws below stay inside these ranges and needn't reach their ends.
Inputs may be any that keep to these rules, and one draw needn't show every extreme that they name: `connections`: each block's neighbour blocks lie among the 16 blocks of its own node index and the one block just before and just after them; links 0 and 1 are the previous and next block (the next and previous at the ends). `counts`: in every sweep some slot takes 5 iterations.
All inputs are finite; a program needn't handle non-finite values.
Results may differ from the reference program's by a relative error of at most 0.0003.
Values sent between devices are 32-bit elements; how exact they have to be, the bound alone decides.
No kernel may reach another device: no remote copies, remote signals or barrier semaphores. Data moves between devices by JAX's collectives and lax.ppermute only.
A program may use at most 64 MiB of HBM per device.

```python
import math
import jax
import jax.numpy as jnp
from jax import lax

F = 64
SAMPLES = 128
LINKS = 4
LMAX = 5
SWEEPS = 2
NODE_BLOCK_COUNT = 16
NB = 256
NODES = 32768


def draw_connections(key, part):
    key = jax.random.fold_in(key, 7)
    blocks = jnp.arange(NB, dtype=jnp.int32)
    starts = blocks // NODE_BLOCK_COUNT * NODE_BLOCK_COUNT
    random_local = jax.random.randint(key, (NB, 2), 0, NODE_BLOCK_COUNT + 2).astype(jnp.int32) + starts[:, None] - 1
    random_local = jnp.clip(random_local, 0, NB - 1)
    before = jnp.where(blocks > 0, blocks - 1, blocks + 1)
    after = jnp.where(blocks < NB - 1, blocks + 1, blocks - 1)
    return jnp.stack([before, after, random_local[:, 0], random_local[:, 1]], axis=1).astype(jnp.int32)


def draw_counts(key, part):
    key = jax.random.fold_in(key, 11)
    first_key, second_key = jax.random.split(key)
    base = jax.random.randint(first_key, (SWEEPS, F), 1, LMAX + 1).astype(jnp.int32)
    picked = jax.random.randint(second_key, (SWEEPS, 1), 0, F).astype(jnp.int32)
    slots = jnp.arange(F, dtype=jnp.int32)[None, :]
    return jnp.where(slots == picked, LMAX, base).astype(jnp.int32)


def block_levels(stream_key, dims, cuts, least, high):
    loudness = 1.0
    for position, parts in cuts:
        draws = jax.random.uniform(jax.random.fold_in(jax.random.fold_in(stream_key, 6), position), (parts,), jnp.float32, least / len(cuts), high / len(cuts))
        loudness = loudness * jnp.repeat(jnp.exp(draws), dims[position] // parts).reshape((-1,) + (1,) * (len(dims) - 1 - position))
    return loudness


def noise(stream_key, dims, deviation, reach, pieces=(), kind=jnp.bfloat16):
    entries = jax.random.normal(stream_key, dims, jnp.float32) * deviation
    if len(pieces) > 0:
        entries = block_levels(stream_key, dims, pieces, -0.22, 0.18) * entries
    return jnp.clip(entries, min=-reach, max=reach).astype(kind)


def setup_inputs(seed: int = 0) -> dict:
    splits = jax.random.split(jax.random.key(seed), 11)
    harmonics = noise(splits[0], (F, 2, 3, NODES), 1.0, 6.0, ((0, 16), (3, 16)), jnp.float32)
    forcing = noise(splits[1], (F, 2, 3, NODES), 1.0, 6.0, ((0, 16), (3, 16)), jnp.float32)
    depths = jnp.clip(jnp.exp(math.log(8.0) - 2.0794415 * jax.random.uniform(splits[2], (NODES,), jnp.float32) ** block_levels(splits[2], (NODES,), ((0, 16),), -0.2, 0.2)), 1.0, 8.0)
    damping = jnp.clip(jnp.exp(math.log(2.0) - 2.3025851 * jax.random.uniform(splits[3], (NODES,), jnp.float32) ** block_levels(splits[3], (NODES,), ((0, 16),), -0.2, 0.2)), 0.2, 2.0)
    weights = jnp.clip(jnp.exp(math.log(1.0) - 2.3025851 * jax.random.uniform(splits[4], (LINKS, NODES), jnp.float32) ** block_levels(splits[4], (LINKS, NODES), ((1, 16),), -0.2, 0.2)), 0.1, 1.0)
    couple_east = jnp.clip(jax.random.uniform(splits[5], (LINKS, NODES), jnp.float32, -0.3, 0.3) * block_levels(splits[5], (LINKS, NODES), ((1, 16),), -0.4, 0.0), -0.3, 0.3)
    couple_north = jnp.clip(jax.random.uniform(splits[6], (LINKS, NODES), jnp.float32, -0.3, 0.3) * block_levels(splits[6], (LINKS, NODES), ((1, 16),), -0.4, 0.0), -0.3, 0.3)
    connections = draw_connections(jax.random.fold_in(splits[10], 71), 0)
    counts = draw_counts(jax.random.fold_in(splits[10], 71), 0)
    harmonic_of_slot = jax.random.permutation(splits[9], F).astype(jnp.int32)
    return {"harmonics": harmonics, "forcing": forcing, "depths": depths, "damping": damping, "weights": weights, "couple_east": couple_east, "couple_north": couple_north, "connections": connections, "counts": counts, "harmonic_of_slot": harmonic_of_slot}


FRICTION = 2.0
CORIOLIS = 0.5
ETA_DAMP = 0.2
OMEGA_STEP = 0.05
SPEED_FLOOR = 0.01
TOP_HARMONIC = lax.Precision.HIGHEST

def harmonic_tables(harmonic_of_slot, sample_total):
    sample_moments = jnp.arange(sample_total, dtype=jnp.int32)
    pointwise_products = sample_moments[:, None] * harmonic_of_slot[None, :] % sample_total
    angles = pointwise_products.astype(jnp.float32) * (2.0 * math.pi / sample_total)
    cosine = jnp.cos(angles)
    sines = jnp.sin(angles)
    slots = harmonic_of_slot.shape[0]
    synthesis = jnp.stack([cosine, -sines], axis=2).reshape(sample_total, 2 * slots)
    weighting = jnp.where(harmonic_of_slot == 0, 1.0, 2.0).astype(jnp.float32) / sample_total
    analysis = jnp.stack([cosine * weighting, -sines * weighting], axis=2).reshape(sample_total, 2 * slots).T
    return (synthesis, analysis)

def friction_terms(fields, depth_cols, synthesis, analysis):
    slots = fields.shape[0]
    columns = fields.shape[3]
    fields_at_moments = jnp.dot(synthesis, fields.reshape(2 * slots, 3 * columns), precision=TOP_HARMONIC)
    fields_at_moments = fields_at_moments.reshape(-1, 3, columns)
    elevation = fields_at_moments[:, 0]
    eastward = fields_at_moments[:, 1]
    northward = fields_at_moments[:, 2]
    column_depth = depth_cols + 0.5 * jnp.tanh(elevation)
    magnitude = jnp.sqrt(eastward * eastward + northward * northward + SPEED_FLOOR)
    factor = FRICTION * magnitude / column_depth
    stacked = jnp.stack([factor * eastward, factor * northward], axis=1).reshape(-1, 2 * columns)
    return jnp.dot(analysis, stacked, precision=TOP_HARMONIC).reshape(slots, 2, 2, columns)

def assemble(fields, beside_of, angular, damping, weights, couple_east, couple_north):
    spread = jnp.zeros_like(fields)
    inflow = jnp.zeros_like(fields[:, :, 0])
    grad_east = jnp.zeros_like(inflow)
    northern_gradient = jnp.zeros_like(inflow)
    for link in range(weights.shape[0]):
        change = beside_of(link) - fields
        spread = spread - weights[link] * change
        inflow = inflow + couple_east[link] * change[:, :, 1] + couple_north[link] * change[:, :, 2]
        grad_east = grad_east + couple_east[link] * change[:, :, 0]
        northern_gradient = northern_gradient + couple_north[link] * change[:, :, 0]
    damping_rows = jnp.stack([ETA_DAMP * jnp.ones_like(damping), damping, damping])
    coupled = jnp.stack([inflow, grad_east - CORIOLIS * fields[:, :, 2], northern_gradient + CORIOLIS * fields[:, :, 1]], axis=2)
    rotation = angular[:, None, None, None] * jnp.stack([-fields[:, 1], fields[:, 0]], axis=1)
    return damping_rows * fields + spread + coupled + rotation

def complex_scale(alpha_real, alpha_imag, values):
    scale_real = alpha_real[:, None, None]
    scale_imag = alpha_imag[:, None, None]
    real_part = scale_real * values[:, 0] - scale_imag * values[:, 1]
    imag_part = scale_real * values[:, 1] + scale_imag * values[:, 0]
    return jnp.stack([real_part, imag_part], axis=1)

def reference(harmonics, forcing, depths, damping, weights, couple_east, couple_north, connections, counts, harmonic_of_slot):
    synthesis, analysis = harmonic_tables(harmonic_of_slot, SAMPLES)
    angular = OMEGA_STEP * harmonic_of_slot.astype(jnp.float32)
    blocks = connections.shape[0]

    def operate(fields):
        blocked = fields.reshape(F, 2, 3, blocks, 128)

        def beside_of(link):
            return jnp.take(blocked, connections[:, link], axis=3).reshape(fields.shape)
        return assemble(fields, beside_of, angular, damping, weights, couple_east, couple_north)
    fields = harmonics
    residual = forcing
    for sweep_index in range(SWEEPS):
        friction = friction_terms(fields, depths, synthesis, analysis)
        friction = jnp.concatenate([jnp.zeros_like(friction[:, :, :1]), friction], axis=2)
        residual = forcing - friction - operate(fields)
        for inner in range(LMAX):
            image = operate(residual)
            upper_real = lax.optimization_barrier(jnp.sum(image[:, 0] * residual[:, 0] + image[:, 1] * residual[:, 1], axis=(1, 2)))
            upper_imag = lax.optimization_barrier(jnp.sum(image[:, 0] * residual[:, 1] - image[:, 1] * residual[:, 0], axis=(1, 2)))
            lower = lax.optimization_barrier(jnp.sum(image[:, 0] * image[:, 0] + image[:, 1] * image[:, 1], axis=(1, 2))) + 1e-06
            active = (inner < counts[sweep_index]).astype(jnp.float32)
            alpha_real = active * upper_real / lower
            alpha_imag = active * upper_imag / lower
            fields = fields + complex_scale(alpha_real, alpha_imag, residual)
            residual = residual - complex_scale(alpha_real, alpha_imag, image)
    return (fields, residual)
```

```python
import functools
import math

import jax
import jax.numpy as jnp
import numpy as np
from jax import lax
from jax.experimental import pallas as pl
from jax.experimental.pallas import tpu as pltpu
from jax.sharding import PartitionSpec as P

SAMPLES = 128
LMAX = 5
SWEEPS = 2

FRICTION = 2.0
CORIOLIS = 0.5
ETA_DAMP = 0.2
OMEGA_STEP = 0.05
SPEED_FLOOR = 0.01
TOP_HARMONIC = lax.Precision.HIGHEST

RANKS = 16
LANES = 128
SHARE = 8
SHIFT = 2.5
COUNT = LMAX + 1
REAL_PAIRS = [(m, n) for m in range(COUNT) for n in range(m, COUNT)]
IMAG_PAIRS = [(m, n) for m in range(COUNT) for n in range(m + 1, COUNT)]
ROW_DAMPING, ROW_DEPTHS, ROW_LINKS = 12, 13, 14

VMEM = pl.BlockSpec(memory_space=pltpu.VMEM)
HBM = pl.BlockSpec(memory_space=pl.ANY)
SMEM = pl.BlockSpec(memory_space=pltpu.SMEM)


def iota(shape, axis):
    return lax.broadcasted_iota(jnp.int32, shape, axis)


def swap_blocks(rows):
    lane = iota((8, LANES), 1)
    rows = list(rows)
    for bit in range(4):
        step = SHARE << bit
        upper = (lane & step) != 0
        for i in range(RANKS):
            if i & (1 << bit):
                continue
            low, high = rows[i], rows[i | (1 << bit)]
            rows[i] = jnp.where(upper, pltpu.roll(high, step, 1), low)
            rows[i | (1 << bit)] = jnp.where(upper, high, pltpu.roll(low, LANES - step, 1))
    return rows


def pack_group(rows_of, out_ref, group):
    rows = [rows_of(b) for b in range(RANKS)]
    for rank, row in enumerate(swap_blocks(rows)):
        out_ref[rank, group] = row


def pack_kernel(
    fields_hbm,
    forcing_hbm,
    weights_hbm,
    east_hbm,
    north_hbm,
    damping_hbm,
    depths_hbm,
    links_ref,
    out_ref,
    fields_ref,
    forcing_ref,
    weights_ref,
    east_ref,
    north_ref,
    damping_ref,
    depths_ref,
    rows_ref,
    sems,
):
    sources = (fields_hbm, forcing_hbm, weights_hbm, east_hbm, north_hbm, damping_hbm, depths_hbm)
    targets = (fields_ref, forcing_ref, weights_ref, east_ref, north_ref, damping_ref, depths_ref)
    copies = [pltpu.make_async_copy(a, b, sems.at[i]) for i, (a, b) in enumerate(zip(sources, targets))]
    for copy in copies:
        copy.start()
    first = lax.axis_index("node") * RANKS
    for link in range(2):
        for b in range(RANKS):
            local = (links_ref[2 + link, b] - first).astype(jnp.float32)
            at = ROW_LINKS + link
            rows_ref[at, :, LANES * b : LANES * (b + 1)] = jnp.full((1, LANES), local, jnp.float32)
    for group in range(6):
        if group % 3 == 0:
            copies[group // 3].wait()
        source = (fields_ref, forcing_ref)[group // 3]

        def block(b):
            start = 32 * (group % 3) + 2 * b
            parts = [source[pl.ds(start + part, 4, stride=96), :] for part in range(2)]
            return jnp.concatenate(parts, axis=0)

        pack_group(block, out_ref, group)
    for copy in copies[2:]:
        copy.wait()
    for kind, source in enumerate((weights_ref, east_ref, north_ref)):
        for link in range(4):
            rows_ref[4 * kind + link] = source[link : link + 1, :]
    rows_ref[ROW_DAMPING] = damping_ref[...]
    rows_ref[ROW_DEPTHS] = depths_ref[...]
    mine = lax.axis_index("freq")
    pack_group(lambda b: jnp.broadcast_to(rows_ref[mine, :, LANES * b : LANES * (b + 1)], (8, LANES)), out_ref, 6)


def forward_kernel(given_ref, out_ref):
    for half in range(2):
        rows = jnp.concatenate([given_ref[8 * half + i, 6, 0:1] for i in range(8)], axis=0)
        for rank in range(RANKS):
            out_ref[rank, 3 + half] = rows
    for rank in range(RANKS):
        for comp in range(3):
            out_ref[rank, comp] = given_ref[rank, comp]


def unpack_kernel(x_ref, fields_ref, residual_ref):
    for group in range(6):
        target = fields_ref if group < 3 else residual_ref
        comp = group % 3
        rows = swap_blocks([x_ref[rank, group] for rank in range(RANKS)])
        for b, row in enumerate(rows):
            for part in range(2):
                target[pl.ds(32 * comp + 2 * b + part, 4, stride=96), :] = row[4 * part : 4 * part + 4]


def tables_kernel(harmonic_ref, cosines_ref, synthesis_ref, analysis_ref):
    samples = iota((SAMPLES, LANES), 0)
    quarter = jnp.where((iota((SAMPLES, LANES), 1) & 4) != 0, SAMPLES // 4, 0)
    harmonic = jnp.broadcast_to(harmonic_ref[...], (SAMPLES, LANES))
    turn = (samples * harmonic + quarter) & (SAMPLES - 1)
    cosines = jnp.broadcast_to(cosines_ref[...], (SAMPLES, LANES))
    synthesis = jnp.take_along_axis(cosines, turn, axis=1, mode="promise_in_bounds")
    synthesis_ref[...] = synthesis
    analysis_ref[...] = (synthesis * jnp.where(harmonic == 0, 1.0 / SAMPLES, 2.0 / SAMPLES)).T


def friction_kernel(x_ref, table_ref, synthesis_ref, analysis_ref, out_ref):
    moments = [
        jnp.dot(
            synthesis_ref[...],
            x_ref[:, comp].reshape(LANES, LANES),
            precision=TOP_HARMONIC,
            preferred_element_type=jnp.float32,
        )
        for comp in range(3)
    ]
    elevation, eastward, northward = moments
    group = lax.axis_index("freq")
    depths = table_ref[ROW_DEPTHS, 3 + group // 8]
    depth = jnp.sum(jnp.where(iota((8, LANES), 0) == group % 8, depths, 0.0), axis=0, keepdims=True)
    column_depth = depth + 0.5 * jnp.tanh(elevation)
    magnitude = jnp.sqrt(eastward * eastward + northward * northward + SPEED_FLOOR)
    factor = FRICTION * magnitude / column_depth
    for comp, moving in enumerate((eastward, northward)):
        terms = jnp.dot(
            analysis_ref[...], factor * moving, precision=TOP_HARMONIC, preferred_element_type=jnp.float32
        )
        out_ref[:, comp] = terms.reshape(RANKS, 8, LANES)


def prepare_links(table_ref, links_ref, index_ref):
    share = iota((8, LANES), 1) & (SHARE - 1)
    for half in range(2):
        rows = [table_ref[at, 3 + half] for at in range(RANKS)]
        spread = rows[0] + rows[1] + rows[2] + rows[3]
        values = rows[:12] + [
            spread + (ETA_DAMP - SHIFT),
            spread + (rows[ROW_DAMPING] - SHIFT),
            rows[4] + rows[5] + rows[6] + rows[7],
            rows[8] + rows[9] + rows[10] + rows[11],
        ]
        for i in range(8):
            for at, value in enumerate(values):
                links_ref[8 * half + i, at] = jnp.broadcast_to(value[i : i + 1], (8, LANES))
        for link in range(2):
            at = rows[ROW_LINKS + link].astype(jnp.int32)
            outside = jnp.logical_or(at < 0, at > RANKS - 1)
            lane = (at & (RANKS - 1)) * SHARE + share
            index = jnp.where(outside, lane + LANES, lane)
            for i in range(8):
                index_ref[8 * half + i, link] = jnp.broadcast_to(index[i : i + 1], (8, LANES))


def apply_operator(vectors, links_ref, index_ref):
    lane = iota((8, LANES), 1)
    first = lane < SHARE
    last = lane >= LANES - SHARE
    result = []
    for g in range(RANKS):
        here = vectors[g]
        before = vectors[g - 1] if g > 0 else [pltpu.roll(x, LANES - 2 * SHARE, 1) for x in here]
        after = vectors[g + 1] if g < RANKS - 1 else [pltpu.roll(x, 2 * SHARE, 1) for x in here]
        beside = []
        beside.append([pltpu.roll(jnp.where(last, p, x), SHARE, 1) for p, x in zip(before, here)])
        beside.append([pltpu.roll(jnp.where(first, n, x), LANES - SHARE, 1) for n, x in zip(after, here)])
        edges = [jnp.where(last, p, n) for p, n in zip(before, after)]
        for link in range(2):
            index = index_ref[g, link]
            outside = index >= LANES
            index = index & (LANES - 1)
            beside.append(
                [
                    jnp.where(
                        outside,
                        jnp.take_along_axis(e, index, axis=1, mode="promise_in_bounds"),
                        jnp.take_along_axis(x, index, axis=1, mode="promise_in_bounds"),
                    )
                    for e, x in zip(edges, here)
                ]
            )
        x_ele, x_east, x_north = here
        eta_sum, flow_sum, east_sum, north_sum = [links_ref[g, 12 + at] for at in range(4)]
        ele = eta_sum * x_ele - east_sum * x_east - north_sum * x_north
        east = flow_sum * x_east - east_sum * x_ele - CORIOLIS * x_north
        north = flow_sum * x_north - north_sum * x_ele + CORIOLIS * x_east
        for link in range(4):
            y_ele, y_east, y_north = beside[link]
            weight, to_east, to_north = [links_ref[g, at + link] for at in (0, 4, 8)]
            ele = ele - weight * y_ele + to_east * y_east + to_north * y_north
            east = east - weight * y_east + to_east * y_ele
            north = north - weight * y_north + to_north * y_ele
        result.append([ele, east, north])
    return result


def slot_rows(ref, pick):
    first = lax.axis_index("freq") * 4
    slot = iota((8, LANES), 0) & 3
    values = [pick(ref, first + s) for s in range(4)]
    return jnp.where(slot == 0, values[0], jnp.where(slot == 1, values[1], jnp.where(slot == 2, values[2], values[3])))


def angular_rows(harmonic_ref):
    return OMEGA_STEP * slot_rows(harmonic_ref, lambda ref, i: ref[i]).astype(jnp.float32)


def start_kernel(given_ref, table_ref, harmonic_ref, base_ref, links_ref, index_ref):
    prepare_links(table_ref, links_ref, index_ref)
    turn = angular_rows(harmonic_ref) * jnp.where(iota((8, LANES), 0) < 4, -1.0, 1.0)
    vectors = [[given_ref[g, comp] for comp in range(3)] for g in range(RANKS)]
    images = apply_operator(vectors, links_ref, index_ref)
    for g in range(RANKS):
        for comp in range(3):
            rest = SHIFT * vectors[g][comp] + turn * pltpu.roll(vectors[g][comp], 4, 0)
            base_ref[g, comp] = given_ref[g, 3 + comp] - images[g][comp] - rest


def basis_kernel(base_ref, friction_ref, links_ref, index_ref, basis_ref, gram_ref):
    for g in range(RANKS):
        basis_ref[0, g, 0] = base_ref[g, 0]
        basis_ref[0, g, 1] = base_ref[g, 1] - friction_ref[g, 0]
        basis_ref[0, g, 2] = base_ref[g, 2] - friction_ref[g, 1]

    def power(m, _):
        vectors = [[basis_ref[m, g, comp] for comp in range(3)] for g in range(RANKS)]
        images = apply_operator(vectors, links_ref, index_ref)
        for g in range(RANKS):
            for comp in range(3):
                basis_ref[m + 1, g, comp] = images[g][comp]
        return 0

    lax.fori_loop(0, LMAX, power, 0)

    def products(g, sums):
        for comp in range(3):
            vectors = [basis_ref[m, g, comp] for m in range(COUNT)]
            turned = [None] + [pltpu.roll(v, 4, 0) for v in vectors[1:]]
            terms = [vectors[m] * vectors[n] for m, n in REAL_PAIRS]
            terms += [vectors[m] * turned[n] for m, n in IMAG_PAIRS]
            sums = tuple(a + b for a, b in zip(sums, terms))
        return sums

    entries = len(REAL_PAIRS) + len(IMAG_PAIRS)
    sums = lax.fori_loop(0, RANKS, products, tuple(jnp.zeros((8, LANES), jnp.float32) for _ in range(entries)))
    lane = iota((8, LANES), 1)
    gram = jnp.zeros((8, LANES), jnp.float32)
    for entry, value in enumerate(sums):
        gram = jnp.where(lane == entry, jnp.sum(value, axis=1, keepdims=True), gram)
    turned = pltpu.roll(gram, 4, 0)
    gram = jnp.where(lane < len(REAL_PAIRS), gram + turned, gram - turned)
    packed = jnp.where(lane < LANES // 2, gram, pltpu.roll(pltpu.roll(gram, LANES // 2, 1), 6, 0))[:2]
    for rank in range(RANKS):
        gram_ref[rank] = packed


def step_sizes(gram_ref, harmonic_ref, counts_ref, sweep):
    gram = gram_ref[0]
    for rank in range(1, RANKS):
        gram = gram + gram_ref[rank]
    swapped = pltpu.roll(gram, LANES // 2, 1)
    gram = jnp.concatenate([gram, swapped, gram, swapped], axis=0)

    def entry(values, at):
        return jnp.broadcast_to(values[:, at : at + 1], (8, LANES))

    inner = {}
    for at, (m, n) in enumerate(REAL_PAIRS):
        inner[m, n] = (entry(gram, at), None)
    for at, (m, n) in enumerate(IMAG_PAIRS):
        inner[m, n] = (inner[m, n][0], entry(gram, len(REAL_PAIRS) + at))

    def mul(a, b):
        return (a[0] * b[0] - a[1] * b[1], a[0] * b[1] + a[1] * b[0])

    def add(a, b):
        return (a[0] + b[0], a[1] + b[1])

    def conj_mul(a, b):
        return (a[0] * b[0] + a[1] * b[1], a[0] * b[1] - a[1] * b[0])

    def gram_times(m, n, b):
        if m == n:
            g = inner[m, n][0]
            return (g * b[0], g * b[1])
        if m < n:
            return mul(inner[m, n], b)
        return conj_mul(inner[n, m], b)

    angular = angular_rows(harmonic_ref)
    counts = slot_rows(counts_ref, lambda ref, i: ref[sweep, i])
    zero = jnp.zeros((8, LANES), jnp.float32)
    residual = [(jnp.ones((8, LANES), jnp.float32), zero)]
    correction = [(zero, zero) for _ in range(LMAX)]
    for step in range(LMAX):
        image = []
        for m in range(step + 2):
            value = (zero, zero)
            if m <= step:
                r = residual[m]
                value = (SHIFT * r[0] - angular * r[1], SHIFT * r[1] + angular * r[0])
            if m > 0:
                value = add(value, residual[m - 1])
            image.append(value)
        upper = (zero, zero)
        lower = zero
        for m in range(step + 2):
            with_residual = (zero, zero)
            for n in range(step + 1):
                with_residual = add(with_residual, gram_times(m, n, residual[n]))
            upper = add(upper, conj_mul(image[m], with_residual))
            with_image = (zero, zero)
            for n in range(step + 2):
                with_image = add(with_image, gram_times(m, n, image[n]))
            lower = lower + image[m][0] * with_image[0] + image[m][1] * with_image[1]
        lower = lower + 1e-06
        active = jnp.where(step < counts, 1.0, 0.0)
        alpha = (active * upper[0] / lower, active * upper[1] / lower)
        for m in range(step + 1):
            correction[m] = add(correction[m], mul(alpha, residual[m]))
        residual = residual + [(zero, zero)]
        for m in range(step + 2):
            change = mul(alpha, image[m])
            residual[m] = (residual[m][0] - change[0], residual[m][1] - change[1])
    return correction, residual


def combine(coefs, vectors, sign):
    straight = coefs[0][0] * vectors[0]
    turned = coefs[0][1] * vectors[0]
    for (real, imag), vector in zip(coefs[1:], vectors[1:]):
        straight = straight + real * vector
        turned = turned + imag * vector
    return straight + sign * pltpu.roll(turned, 4, 0)


def update_kernel(sweep, gram_ref, fields_ref, basis_ref, friction_ref, harmonic_ref, counts_ref, *outs):
    correction, residual = step_sizes(gram_ref, harmonic_ref, counts_ref, sweep)
    sign = jnp.where(iota((8, LANES), 0) < 4, -1.0, 1.0)

    def update(g, _):
        for comp in range(3):
            vectors = [basis_ref[m, g, comp] for m in range(COUNT)]
            fields = fields_ref[g, comp] + combine(correction, vectors[:LMAX], sign)
            left = combine(residual, vectors, sign)
            if sweep == SWEEPS - 1:
                outs[0][g, comp] = fields
                outs[0][g, 3 + comp] = left
            else:
                outs[0][g, comp] = fields
                outs[1][g, comp] = left if comp == 0 else left + friction_ref[g, comp - 1]
        return 0

    lax.fori_loop(0, RANKS, update, 0)


def struct(*shape):
    return jax.ShapeDtypeStruct(shape, jnp.float32)


def call(kernel, out, specs, scratch=(), mebibytes=16):
    outs = out if isinstance(out, list) else [out]
    result = pl.pallas_call(
        kernel,
        out_shape=outs,
        in_specs=specs,
        out_specs=[VMEM] * len(outs),
        scratch_shapes=list(scratch),
        compiler_params=pltpu.CompilerParams(vmem_limit_bytes=mebibytes * 1024 * 1024),
    )
    return (lambda *args: result(*args)) if isinstance(out, list) else (lambda *args: result(*args)[0])


def exchange(values, axis):
    return lax.all_to_all(values, axis, split_axis=0, concat_axis=0, tiled=True)


def rows_of(x):
    return x.transpose(0, 2, 1, 3).reshape(4, 3, 2, RANKS, LANES).transpose(0, 1, 3, 2, 4).reshape(-1, LANES)


def fields_of(rows):
    return rows.reshape(4, 3, RANKS, 2, LANES).transpose(0, 3, 1, 2, 4).reshape(4, 2, 3, RANKS * LANES)


def body(
    harmonics, forcing, depths, damping, weights, couple_east, couple_north, connections, counts, harmonic_of_slot
):
    whole = pltpu.VMEM((384, LANES), jnp.float32)
    four = pltpu.VMEM((4, 2048), jnp.float32)
    line = pltpu.VMEM((1, 2048), jnp.float32)
    packed = call(
        pack_kernel,
        struct(RANKS, 7, 8, LANES),
        [HBM] * 7 + [SMEM],
        (
            whole,
            whole,
            four,
            four,
            four,
            line,
            line,
            pltpu.VMEM((RANKS, 1, 2048), jnp.float32),
            pltpu.SemaphoreType.DMA((7,)),
        ),
        58,
    )(
        rows_of(harmonics),
        rows_of(forcing),
        weights,
        couple_east,
        couple_north,
        damping.reshape(1, -1),
        depths.reshape(1, -1),
        connections.T,
    )
    given = exchange(packed, "node")
    table = exchange(call(forward_kernel, struct(RANKS, 5, 8, LANES), [VMEM])(given), "freq")

    slots = jnp.broadcast_to(harmonic_of_slot.reshape(RANKS, 1, 4), (RANKS, 2, 4)).reshape(1, LANES)
    cosines = np.cos(np.arange(SAMPLES) * (2.0 * math.pi / SAMPLES)).astype(np.float32).reshape(1, SAMPLES)

    synthesis, analysis = call(tables_kernel, [struct(SAMPLES, LANES), struct(LANES, SAMPLES)], [VMEM] * 2)(
        slots, cosines
    )

    def friction_of(received):
        terms = call(friction_kernel, struct(RANKS, 2, 8, LANES), [VMEM] * 4)(received, table, synthesis, analysis)
        return exchange(terms, "freq")

    base, links, index = call(
        start_kernel,
        [
            struct(RANKS, 3, 8, LANES),
            struct(RANKS, 16, 8, LANES),
            jax.ShapeDtypeStruct((RANKS, 2, 8, LANES), jnp.int32),
        ],
        [VMEM, VMEM, SMEM],
    )(given, table, harmonic_of_slot)
    fields = given
    friction = friction_of(table)
    for sweep in range(SWEEPS):
        basis, gram = call(
            basis_kernel, [struct(COUNT, RANKS, 3, 8, LANES), struct(RANKS, 2, LANES)], [VMEM] * 4
        )(base, friction, links, index)
        gram = exchange(gram, "node")
        if sweep < SWEEPS - 1:
            outs = [struct(RANKS, 3, 8, LANES), struct(RANKS, 3, 8, LANES)]
        else:
            outs = [struct(RANKS, 6, 8, LANES)]
        results = call(functools.partial(update_kernel, sweep), outs, [VMEM] * 4 + [SMEM] * 2)(
            gram, fields, basis, friction, harmonic_of_slot, counts
        )
        if sweep < SWEEPS - 1:
            fields, base = results
            friction = friction_of(exchange(fields, "freq"))
    out = [struct(384, LANES)] * 2
    fields, residual = call(unpack_kernel, out, [VMEM])(exchange(results[0], "node"))
    return (fields_of(fields), fields_of(residual))


def solution(mesh):
    return jax.shard_map(
        body,
        mesh=mesh,
        in_specs=(
            P("freq", None, None, "node"),
            P("freq", None, None, "node"),
            P("node"),
            P("node"),
            P(None, "node"),
            P(None, "node"),
            P(None, "node"),
            P("node", None),
            P(),
            P(),
        ),
        out_specs=(P("freq", None, None, "node"), P("freq", None, None, "node")),
        check_vma=False,
    )
```

```python
import functools
import math

import jax
import jax.numpy as jnp
import numpy as np
from jax import lax
from jax.experimental import pallas as pl
from jax.experimental.pallas import tpu as pltpu
from jax.sharding import PartitionSpec as P

SAMPLES = 128
LMAX = 5
SWEEPS = 2

FRICTION = 2.0
CORIOLIS = 0.5
ETA_DAMP = 0.2
OMEGA_STEP = 0.05
SPEED_FLOOR = 0.01
TOP_HARMONIC = lax.Precision.HIGHEST

RANKS = 16
LANES = 128
SHARE = 8
SHIFT = 2.5
COUNT = LMAX + 1
REAL_PAIRS = [(m, n) for m in range(COUNT) for n in range(m, COUNT)]
IMAG_PAIRS = [(m, n) for m in range(COUNT) for n in range(m + 1, COUNT)]
ROW_DAMPING, ROW_DEPTHS, ROW_LINKS = 12, 13, 14

FIELDS_AT, COEFS_AT, FRICTION_AT = 3, 6, 8

VMEM = pl.BlockSpec(memory_space=pltpu.VMEM)
HBM = pl.BlockSpec(memory_space=pl.ANY)
SMEM = pl.BlockSpec(memory_space=pltpu.SMEM)


def iota(shape, axis):
    return lax.broadcasted_iota(jnp.int32, shape, axis)


def swap_blocks(rows):
    lane = iota((8, LANES), 1)
    rows = list(rows)
    for bit in range(4):
        step = SHARE << bit
        upper = (lane & step) != 0
        for i in range(RANKS):
            if i & (1 << bit):
                continue
            low, high = rows[i], rows[i | (1 << bit)]
            rows[i] = jnp.where(upper, pltpu.roll(high, step, 1), low)
            rows[i | (1 << bit)] = jnp.where(upper, high, pltpu.roll(low, LANES - step, 1))
    return rows


def read_rows(ref, comp, block):
    start = 32 * comp + 2 * block
    return jnp.concatenate([ref[pl.ds(start + part, 4, stride=96), :] for part in range(2)], axis=0)


def first_kernel(fields_hbm, out_ref, fields_ref, sem):
    copy = pltpu.make_async_copy(fields_hbm, fields_ref, sem)
    copy.start()
    copy.wait()
    for block in range(RANKS):
        for comp in range(3):
            out_ref[block, comp] = read_rows(fields_ref, comp, block)


def pack_kernel(
    fields_hbm,
    forcing_hbm,
    weights_hbm,
    east_hbm,
    north_hbm,
    damping_hbm,
    depths_hbm,
    links_ref,
    _,
    out_ref,
    depth_ref,
    fields_ref,
    forcing_ref,
    weights_ref,
    east_ref,
    north_ref,
    damping_ref,
    depths_ref,
    rows_ref,
    sems,
):
    sources = (fields_hbm, forcing_hbm, weights_hbm, east_hbm, north_hbm, damping_hbm, depths_hbm)
    targets = (fields_ref, forcing_ref, weights_ref, east_ref, north_ref, damping_ref, depths_ref)
    copies = [pltpu.make_async_copy(a, b, sems.at[i]) for i, (a, b) in enumerate(zip(sources, targets))]
    for copy in copies:
        copy.start()
    node = lax.axis_index("node")
    for link in range(2):
        for b in range(RANKS):
            local = (links_ref[2 + link, b] - node * RANKS).astype(jnp.float32)
            at = ROW_LINKS + link
            rows_ref[at : at + 1, LANES * b : LANES * (b + 1)] = jnp.full((1, LANES), local, jnp.float32)
    for copy in copies:
        copy.wait()
    rows_ref[0:4, :] = weights_ref[...]
    rows_ref[4:8, :] = east_ref[...]
    rows_ref[8:12, :] = north_ref[...]
    rows_ref[ROW_DAMPING : ROW_DAMPING + 1, :] = damping_ref[...]
    rows_ref[ROW_DEPTHS : ROW_DEPTHS + 1, :] = depths_ref[...]
    mine = lax.axis_index("freq")
    depth_ref[...] = depths_ref[:, pl.ds(pl.multiple_of(mine * LANES, LANES), LANES)]
    for group in range(8):
        if group < 6:
            rows = [read_rows((forcing_ref, fields_ref)[group // 3], group % 3, b) for b in range(RANKS)]
        else:
            at = 8 * (group - 6)
            rows = [rows_ref[at : at + 8, LANES * b : LANES * (b + 1)] for b in range(RANKS)]
        for rank, row in enumerate(swap_blocks(rows)):
            out_ref[rank, group] = row


def turn_kernel(friction_ref, packed_ref, out_ref):
    for rank in range(RANKS):
        out_ref[rank, 0] = packed_ref[rank, 0]
        for group in range(3, 8):
            out_ref[rank, group] = packed_ref[rank, group]
    for comp in range(2):
        rows = swap_blocks([friction_ref[b, comp] for b in range(RANKS)])
        for rank, row in enumerate(rows):
            out_ref[rank, 1 + comp] = packed_ref[rank, 1 + comp] - row
            out_ref[rank, FRICTION_AT + comp] = row


def unpack_kernel(x_ref, fields_ref, residual_ref):
    for group in range(6):
        target = fields_ref if group < 3 else residual_ref
        comp = group % 3
        rows = swap_blocks([x_ref[rank, group] for rank in range(RANKS)])
        for b, row in enumerate(rows):
            for part in range(2):
                target[pl.ds(32 * comp + 2 * b + part, 4, stride=96), :] = row[4 * part : 4 * part + 4]


def tables_kernel(harmonic_ref, cosines_ref, synthesis_ref, analysis_ref):
    samples = iota((SAMPLES, LANES), 0)
    quarter = jnp.where((iota((SAMPLES, LANES), 1) & 4) != 0, SAMPLES // 4, 0)
    harmonic = jnp.broadcast_to(harmonic_ref[...], (SAMPLES, LANES))
    turn = (samples * harmonic + quarter) & (SAMPLES - 1)
    cosines = jnp.broadcast_to(cosines_ref[...], (SAMPLES, LANES))
    synthesis = jnp.take_along_axis(cosines, turn, axis=1, mode="promise_in_bounds")
    synthesis_ref[...] = synthesis
    analysis_ref[...] = (synthesis * jnp.where(harmonic == 0, 1.0 / SAMPLES, 2.0 / SAMPLES)).T


def friction_kernel(x_ref, depth_ref, synthesis_ref, analysis_ref, out_ref):
    moments = [
        jnp.dot(
            synthesis_ref[...],
            x_ref[:, comp].reshape(LANES, LANES),
            precision=TOP_HARMONIC,
            preferred_element_type=jnp.float32,
        )
        for comp in range(3)
    ]
    elevation, eastward, northward = moments
    column_depth = depth_ref[...] + 0.5 * jnp.tanh(elevation)
    magnitude = jnp.sqrt(eastward * eastward + northward * northward + SPEED_FLOOR)
    factor = FRICTION * magnitude / column_depth
    for comp, moving in enumerate((eastward, northward)):
        terms = jnp.dot(
            analysis_ref[...], factor * moving, precision=TOP_HARMONIC, preferred_element_type=jnp.float32
        )
        out_ref[:, comp] = terms.reshape(RANKS, 8, LANES)


def prepare_links(given_ref, links_ref, index_ref):
    share = iota((8, LANES), 1) & (SHARE - 1)

    def prepare(g, _):
        rows = [jnp.broadcast_to(given_ref[g, COEFS_AT + at // 8, at % 8 : at % 8 + 1], (8, LANES)) for at in range(RANKS)]
        spread = rows[0] + rows[1] + rows[2] + rows[3]
        values = rows[:12] + [
            spread + (ETA_DAMP - SHIFT),
            spread + (rows[ROW_DAMPING] - SHIFT),
            rows[4] + rows[5] + rows[6] + rows[7],
            rows[8] + rows[9] + rows[10] + rows[11],
        ]
        for at, value in enumerate(values):
            links_ref[g, at] = value
        for link in range(2):
            at = rows[ROW_LINKS + link].astype(jnp.int32)
            outside = jnp.logical_or(at < 0, at > RANKS - 1)
            lane = (at & (RANKS - 1)) * SHARE + share
            index_ref[g, link] = jnp.where(outside, lane + LANES, lane)
        return 0

    lax.fori_loop(0, RANKS, prepare, 0)


def apply_operator(vectors, links_ref, index_ref):
    lane = iota((8, LANES), 1)
    first = lane < SHARE
    last = lane >= LANES - SHARE
    result = []
    for g in range(RANKS):
        here = vectors[g]
        before = vectors[g - 1] if g > 0 else [pltpu.roll(x, LANES - 2 * SHARE, 1) for x in here]
        after = vectors[g + 1] if g < RANKS - 1 else [pltpu.roll(x, 2 * SHARE, 1) for x in here]
        beside = []
        beside.append([pltpu.roll(jnp.where(last, p, x), SHARE, 1) for p, x in zip(before, here)])
        beside.append([pltpu.roll(jnp.where(first, n, x), LANES - SHARE, 1) for n, x in zip(after, here)])
        edges = [jnp.where(last, p, n) for p, n in zip(before, after)]
        for link in range(2):
            index = index_ref[g, link]
            outside = index >= LANES
            index = index & (LANES - 1)
            beside.append(
                [
                    jnp.where(
                        outside,
                        jnp.take_along_axis(e, index, axis=1, mode="promise_in_bounds"),
                        jnp.take_along_axis(x, index, axis=1, mode="promise_in_bounds"),
                    )
                    for e, x in zip(edges, here)
                ]
            )
        x_ele, x_east, x_north = here
        eta_sum, flow_sum, east_sum, north_sum = [links_ref[g, 12 + at] for at in range(4)]
        ele = eta_sum * x_ele - east_sum * x_east - north_sum * x_north
        east = flow_sum * x_east - east_sum * x_ele - CORIOLIS * x_north
        north = flow_sum * x_north - north_sum * x_ele + CORIOLIS * x_east
        for link in range(4):
            y_ele, y_east, y_north = beside[link]
            weight, to_east, to_north = [links_ref[g, at + link] for at in (0, 4, 8)]
            ele = ele - weight * y_ele + to_east * y_east + to_north * y_north
            east = east - weight * y_east + to_east * y_ele
            north = north - weight * y_north + to_north * y_ele
        result.append([ele, east, north])
    return result


def slot_rows(ref, pick):
    first = lax.axis_index("freq") * 4
    slot = iota((8, LANES), 0) & 3
    values = [pick(ref, first + s) for s in range(4)]
    return jnp.where(slot == 0, values[0], jnp.where(slot == 1, values[1], jnp.where(slot == 2, values[2], values[3])))


def angular_rows(harmonic_ref):
    return OMEGA_STEP * slot_rows(harmonic_ref, lambda ref, i: ref[i]).astype(jnp.float32)


def first_basis_kernel(given_ref, harmonic_ref, basis_ref, gram_ref, links_ref, index_ref, depth_ref):
    prepare_links(given_ref, links_ref, index_ref)
    depth_ref[...] = given_ref[lax.axis_index("freq"), COEFS_AT + 1, ROW_DEPTHS - 8 : ROW_DEPTHS - 7]
    turn = angular_rows(harmonic_ref) * jnp.where(iota((8, LANES), 0) < 4, -1.0, 1.0)
    vectors = [[given_ref[g, FIELDS_AT + comp] for comp in range(3)] for g in range(RANKS)]
    images = apply_operator(vectors, links_ref, index_ref)
    for g in range(RANKS):
        for comp in range(3):
            rest = SHIFT * vectors[g][comp] + turn * pltpu.roll(vectors[g][comp], 4, 0)
            basis_ref[0, g, comp] = given_ref[g, comp] - images[g][comp] - rest
    extend_basis(links_ref, index_ref, basis_ref, gram_ref)


def basis_kernel(base_ref, friction_ref, links_ref, index_ref, basis_ref, gram_ref):
    for g in range(RANKS):
        basis_ref[0, g, 0] = base_ref[g, 0]
        basis_ref[0, g, 1] = base_ref[g, 1] - friction_ref[g, 0]
        basis_ref[0, g, 2] = base_ref[g, 2] - friction_ref[g, 1]
    extend_basis(links_ref, index_ref, basis_ref, gram_ref)


def extend_basis(links_ref, index_ref, basis_ref, gram_ref):
    def power(m, _):
        vectors = [[basis_ref[m, g, comp] for comp in range(3)] for g in range(RANKS)]
        images = apply_operator(vectors, links_ref, index_ref)
        for g in range(RANKS):
            for comp in range(3):
                basis_ref[m + 1, g, comp] = images[g][comp]
        return 0

    lax.fori_loop(0, LMAX, power, 0)

    def products(g, sums):
        for comp in range(3):
            vectors = [basis_ref[m, g, comp] for m in range(COUNT)]
            turned = [None] + [pltpu.roll(v, 4, 0) for v in vectors[1:]]
            terms = [vectors[m] * vectors[n] for m, n in REAL_PAIRS]
            terms += [vectors[m] * turned[n] for m, n in IMAG_PAIRS]
            sums = tuple(a + b for a, b in zip(sums, terms))
        return sums

    entries = len(REAL_PAIRS) + len(IMAG_PAIRS)
    sums = lax.fori_loop(0, RANKS, products, tuple(jnp.zeros((8, LANES), jnp.float32) for _ in range(entries)))
    lane = iota((8, LANES), 1)
    gram = jnp.zeros((8, LANES), jnp.float32)
    for entry, value in enumerate(sums):
        gram = jnp.where(lane == entry, jnp.sum(value, axis=1, keepdims=True), gram)
    turned = pltpu.roll(gram, 4, 0)
    gram = jnp.where(lane < len(REAL_PAIRS), gram + turned, gram - turned)
    packed = jnp.where(lane < LANES // 2, gram, pltpu.roll(pltpu.roll(gram, LANES // 2, 1), 6, 0))[:2]
    for rank in range(RANKS):
        gram_ref[rank] = packed


def step_sizes(gram_ref, harmonic_ref, counts_ref, sweep):
    gram = gram_ref[0]
    for rank in range(1, RANKS):
        gram = gram + gram_ref[rank]
    swapped = pltpu.roll(gram, LANES // 2, 1)
    gram = jnp.concatenate([gram, swapped, gram, swapped], axis=0)

    def entry(values, at):
        return jnp.broadcast_to(values[:, at : at + 1], (8, LANES))

    inner = {}
    for at, (m, n) in enumerate(REAL_PAIRS):
        inner[m, n] = (entry(gram, at), None)
    for at, (m, n) in enumerate(IMAG_PAIRS):
        inner[m, n] = (inner[m, n][0], entry(gram, len(REAL_PAIRS) + at))

    def mul(a, b):
        return (a[0] * b[0] - a[1] * b[1], a[0] * b[1] + a[1] * b[0])

    def add(a, b):
        return (a[0] + b[0], a[1] + b[1])

    def conj_mul(a, b):
        return (a[0] * b[0] + a[1] * b[1], a[0] * b[1] - a[1] * b[0])

    def gram_times(m, n, b):
        if m == n:
            g = inner[m, n][0]
            return (g * b[0], g * b[1])
        if m < n:
            return mul(inner[m, n], b)
        return conj_mul(inner[n, m], b)

    angular = angular_rows(harmonic_ref)
    counts = slot_rows(counts_ref, lambda ref, i: ref[sweep, i])
    zero = jnp.zeros((8, LANES), jnp.float32)
    residual = [(jnp.ones((8, LANES), jnp.float32), zero)]
    correction = [(zero, zero) for _ in range(LMAX)]
    for step in range(LMAX):
        image = []
        for m in range(step + 2):
            value = (zero, zero)
            if m <= step:
                r = residual[m]
                value = (SHIFT * r[0] - angular * r[1], SHIFT * r[1] + angular * r[0])
            if m > 0:
                value = add(value, residual[m - 1])
            image.append(value)
        upper = (zero, zero)
        lower = zero
        for m in range(step + 2):
            with_residual = (zero, zero)
            for n in range(step + 1):
                with_residual = add(with_residual, gram_times(m, n, residual[n]))
            upper = add(upper, conj_mul(image[m], with_residual))
            with_image = (zero, zero)
            for n in range(step + 2):
                with_image = add(with_image, gram_times(m, n, image[n]))
            lower = lower + image[m][0] * with_image[0] + image[m][1] * with_image[1]
        lower = lower + 1e-06
        active = jnp.where(step < counts, 1.0, 0.0)
        alpha = (active * upper[0] / lower, active * upper[1] / lower)
        for m in range(step + 1):
            correction[m] = add(correction[m], mul(alpha, residual[m]))
        residual = residual + [(zero, zero)]
        for m in range(step + 2):
            change = mul(alpha, image[m])
            residual[m] = (residual[m][0] - change[0], residual[m][1] - change[1])
    return correction, residual


def combine(coefs, vectors, sign):
    straight = coefs[0][0] * vectors[0]
    turned = coefs[0][1] * vectors[0]
    for (real, imag), vector in zip(coefs[1:], vectors[1:]):
        straight = straight + real * vector
        turned = turned + imag * vector
    return straight + sign * pltpu.roll(turned, 4, 0)


def update_kernel(sweep, gram_ref, fields_ref, basis_ref, friction_ref, harmonic_ref, counts_ref, *outs):
    correction, residual = step_sizes(gram_ref, harmonic_ref, counts_ref, sweep)
    sign = jnp.where(iota((8, LANES), 0) < 4, -1.0, 1.0)
    fields_at = FIELDS_AT if sweep == 0 else 0

    def update(g, _):
        for comp in range(3):
            vectors = [basis_ref[m, g, comp] for m in range(COUNT)]
            fields = fields_ref[g, fields_at + comp] + combine(correction, vectors[:LMAX], sign)
            left = combine(residual, vectors, sign)
            if sweep == SWEEPS - 1:
                outs[0][g, comp] = fields
                outs[0][g, 3 + comp] = left
            else:
                outs[0][g, comp] = fields
                outs[1][g, comp] = left if comp == 0 else left + friction_ref[g, FRICTION_AT + comp - 1]
        return 0

    lax.fori_loop(0, RANKS, update, 0)


def struct(*shape):
    return jax.ShapeDtypeStruct(shape, jnp.float32)


def call(kernel, out, specs, scratch=(), mebibytes=16, out_specs=None):
    outs = out if isinstance(out, list) else [out]
    result = pl.pallas_call(
        kernel,
        out_shape=outs,
        in_specs=specs,
        out_specs=out_specs or [VMEM] * len(outs),
        scratch_shapes=list(scratch),
        compiler_params=pltpu.CompilerParams(vmem_limit_bytes=mebibytes * 1024 * 1024),
    )
    return (lambda *args: result(*args)) if isinstance(out, list) else (lambda *args: result(*args)[0])


def exchange(values, axis):
    return lax.all_to_all(values, axis, split_axis=0, concat_axis=0, tiled=True)


def rows_of(x):
    return x.transpose(0, 2, 1, 3).reshape(4, 3, 2, RANKS, LANES).transpose(0, 1, 3, 2, 4).reshape(-1, LANES)


def fields_of(rows):
    return rows.reshape(4, 3, RANKS, 2, LANES).transpose(0, 3, 1, 2, 4).reshape(4, 2, 3, RANKS * LANES)


def body(
    harmonics, forcing, depths, damping, weights, couple_east, couple_north, connections, counts, harmonic_of_slot
):
    whole = pltpu.VMEM((384, LANES), jnp.float32)
    four = pltpu.VMEM((4, 2048), jnp.float32)
    line = pltpu.VMEM((1, 2048), jnp.float32)
    fields_rows = rows_of(harmonics)
    first = call(
        first_kernel, struct(RANKS, 3, 8, LANES), [HBM], (whole, pltpu.SemaphoreType.DMA(())), 58
    )(fields_rows)
    received = exchange(first, "freq")

    slots = jnp.broadcast_to(harmonic_of_slot.reshape(RANKS, 1, 4), (RANKS, 2, 4)).reshape(1, LANES)
    cosines = np.cos(np.arange(SAMPLES) * (2.0 * math.pi / SAMPLES)).astype(np.float32).reshape(1, SAMPLES)
    synthesis, analysis = call(tables_kernel, [struct(SAMPLES, LANES), struct(LANES, SAMPLES)], [VMEM] * 2)(
        slots, cosines
    )

    def friction_of(received, depth):
        return call(friction_kernel, struct(RANKS, 2, 8, LANES), [VMEM] * 4)(received, depth, synthesis, analysis)

    packed, depth = call(
        pack_kernel,
        [struct(RANKS, 8, 8, LANES), struct(1, LANES)],
        [HBM] * 7 + [SMEM, HBM],
        (
            whole,
            whole,
            four,
            four,
            four,
            line,
            line,
            pltpu.VMEM((RANKS, 2048), jnp.float32),
            pltpu.SemaphoreType.DMA((7,)),
        ),
        58,
    )(
        fields_rows,
        rows_of(forcing),
        weights,
        couple_east,
        couple_north,
        damping.reshape(1, -1),
        depths.reshape(1, -1),
        connections.T,
        first,
    )
    friction = exchange(friction_of(received, depth), "freq")
    packed = call(turn_kernel, struct(RANKS, 10, 8, LANES), [VMEM] * 2)(friction, packed)
    given = exchange(packed, "node")

    basis_out = [struct(COUNT, RANKS, 3, 8, LANES), struct(RANKS, 2, LANES)]
    links_out = [struct(RANKS, 16, 8, LANES), jax.ShapeDtypeStruct((RANKS, 2, 8, LANES), jnp.int32), struct(1, LANES)]
    basis, gram, links, index, depth = call(first_basis_kernel, basis_out + links_out, [VMEM, SMEM])(
        given, harmonic_of_slot
    )

    def update(sweep, outs, gram, fields, basis):
        return call(functools.partial(update_kernel, sweep), outs, [VMEM] * 4 + [SMEM] * 2)(
            exchange(gram, "node"), fields, basis, given, harmonic_of_slot, counts
        )

    fields, base = update(0, [struct(RANKS, 3, 8, LANES)] * 2, gram, given, basis)
    friction = exchange(friction_of(exchange(fields, "freq"), depth), "freq")
    basis, gram = call(basis_kernel, basis_out, [VMEM] * 4)(base, friction, links, index)
    results = update(1, [struct(RANKS, 6, 8, LANES)], gram, fields, basis)
    out = [struct(384, LANES)] * 2
    fields, residual = call(unpack_kernel, out, [VMEM])(exchange(results[0], "node"))
    return (fields_of(fields), fields_of(residual))


def solution(mesh):
    return jax.shard_map(
        body,
        mesh=mesh,
        in_specs=(
            P("freq", None, None, "node"),
            P("freq", None, None, "node"),
            P("node"),
            P("node"),
            P(None, "node"),
            P(None, "node"),
            P(None, "node"),
            P("node", None),
            P(),
            P(),
        ),
        out_specs=(P("freq", None, None, "node"), P("freq", None, None, "node")),
        check_vma=False,
    )
```

```python
import functools
import math

import jax
import jax.numpy as jnp
import numpy as np
from jax import lax
from jax.experimental import pallas as pl
from jax.experimental.pallas import tpu as pltpu
from jax.sharding import PartitionSpec as P

SAMPLES = 128
LMAX = 5
SWEEPS = 2

FRICTION = 2.0
CORIOLIS = 0.5
ETA_DAMP = 0.2
OMEGA_STEP = 0.05
SPEED_FLOOR = 0.01
TOP_HARMONIC = lax.Precision.HIGHEST

RANKS = 16
LANES = 128
SHARE = 8
COUNT = LMAX + 1
REAL_PAIRS = [(m, n) for m in range(COUNT) for n in range(m, COUNT)]
IMAG_PAIRS = [(m, n) for m in range(COUNT) for n in range(m + 1, COUNT)]
ROW_DAMPING, ROW_DEPTHS, ROW_LINKS = 12, 13, 14

VMEM = pl.BlockSpec(memory_space=pltpu.VMEM)
HBM = pl.BlockSpec(memory_space=pl.ANY)
SMEM = pl.BlockSpec(memory_space=pltpu.SMEM)


def iota(shape, axis):
    return lax.broadcasted_iota(jnp.int32, shape, axis)


def swap_blocks(rows):
    lane = iota((8, LANES), 1)
    rows = list(rows)
    for bit in range(4):
        step = SHARE << bit
        upper = (lane & step) != 0
        for i in range(RANKS):
            if i & (1 << bit):
                continue
            low, high = rows[i], rows[i | (1 << bit)]
            rows[i] = jnp.where(upper, pltpu.roll(high, step, 1), low)
            rows[i | (1 << bit)] = jnp.where(upper, high, pltpu.roll(low, LANES - step, 1))
    return rows


def pack_group(rows_of, out_ref, group):
    rows = [rows_of(b) for b in range(RANKS)]
    for rank, row in enumerate(swap_blocks(rows)):
        out_ref[rank, group] = row


def pack_kernel(
    fields_hbm,
    forcing_hbm,
    weights_hbm,
    east_hbm,
    north_hbm,
    damping_hbm,
    depths_hbm,
    links_ref,
    out_hbm,
    fields_ref,
    forcing_ref,
    weights_ref,
    east_ref,
    north_ref,
    damping_ref,
    depths_ref,
    rows_ref,
    out_ref,
    sems,
    out_sems,
):
    sources = (fields_hbm, forcing_hbm, weights_hbm, east_hbm, north_hbm, damping_hbm, depths_hbm)
    targets = (fields_ref, forcing_ref, weights_ref, east_ref, north_ref, damping_ref, depths_ref)
    copies = [pltpu.make_async_copy(a, b, sems.at[i]) for i, (a, b) in enumerate(zip(sources, targets))]
    for copy in copies:
        copy.start()
    first = lax.axis_index("node") * RANKS
    for link in range(2):
        for b in range(RANKS):
            local = (links_ref[2 + link, b] - first).astype(jnp.float32)
            at = ROW_LINKS + link
            rows_ref[at, :, LANES * b : LANES * (b + 1)] = jnp.full((1, LANES), local, jnp.float32)
    sent = []

    def send(index, group, count):
        part = pl.ds(group, count)
        copy = pltpu.make_async_copy(out_ref.at[:, part], out_hbm.at[:, part], out_sems.at[index])
        copy.start()
        sent.append(copy)

    for group in range(6):
        if group % 3 == 0:
            copies[group // 3].wait()
        source = (fields_ref, forcing_ref)[group // 3]

        def block(b):
            start = 32 * (group % 3) + 2 * b
            parts = [source[pl.ds(start + part, 4, stride=96), :] for part in range(2)]
            return jnp.concatenate(parts, axis=0)

        pack_group(block, out_ref, group)
        if group % 3 == 2:
            send(group // 3, group - 2, 3)
    for copy in copies[2:]:
        copy.wait()
    for kind, source in enumerate((weights_ref, east_ref, north_ref)):
        for link in range(4):
            rows_ref[4 * kind + link] = source[link : link + 1, :]
    rows_ref[ROW_DAMPING] = damping_ref[...]
    rows_ref[ROW_DEPTHS] = depths_ref[...]
    mine = lax.axis_index("freq")
    rows = [jnp.broadcast_to(rows_ref[mine, :, LANES * b : LANES * (b + 1)], (8, LANES)) for b in range(RANKS)]
    diagonal = jnp.sum(weights_ref[...], axis=0, keepdims=True) + (2.0 / 3.0) * damping_ref[...] + ETA_DAMP / 3.0
    mean = jnp.sum(diagonal, axis=1, keepdims=True) * (1.0 / diagonal.shape[1])
    top = iota((8, LANES), 0) == 0
    for rank, row in enumerate(swap_blocks(rows)):
        out_ref[rank, 6] = jnp.where(top, row, mean)
    send(2, 6, 1)
    for copy in sent:
        copy.wait()


def forward_kernel(given_ref, out_ref):
    for half in range(2):
        rows = jnp.concatenate([given_ref[8 * half + i, 6, 0:1] for i in range(8)], axis=0)
        for rank in range(RANKS):
            out_ref[rank, 3 + half] = rows
    for rank in range(RANKS):
        for comp in range(3):
            out_ref[rank, comp] = given_ref[rank, comp]


def unpack_kernel(x_ref, fields_hbm, residual_hbm, fields_ref, residual_ref, sems):
    copies = []
    for i, (target, out) in enumerate(((fields_ref, fields_hbm), (residual_ref, residual_hbm))):
        for comp in range(3):
            rows = swap_blocks([x_ref[rank, 3 * i + comp] for rank in range(RANKS)])
            for b, row in enumerate(rows):
                for part in range(2):
                    target[pl.ds(32 * comp + 2 * b + part, 4, stride=96), :] = row[4 * part : 4 * part + 4]
        copies.append(pltpu.make_async_copy(target, out, sems.at[i]))
        copies[-1].start()
    for copy in copies:
        copy.wait()


def tables_kernel(harmonic_ref, cosines_ref, synthesis_ref, analysis_ref):
    samples = iota((SAMPLES, LANES), 0)
    quarter = jnp.where((iota((SAMPLES, LANES), 1) & 4) != 0, SAMPLES // 4, 0)
    harmonic = jnp.broadcast_to(harmonic_ref[...], (SAMPLES, LANES))
    turn = (samples * harmonic + quarter) & (SAMPLES - 1)
    cosines = jnp.broadcast_to(cosines_ref[...], (SAMPLES, LANES))
    synthesis = jnp.take_along_axis(cosines, turn, axis=1, mode="promise_in_bounds")
    synthesis_ref[...] = synthesis
    analysis_ref[...] = (synthesis * jnp.where(harmonic == 0, 1.0 / SAMPLES, 2.0 / SAMPLES)).T


def friction_kernel(x_ref, table_ref, synthesis_ref, analysis_ref, out_ref):
    moments = [
        jnp.dot(
            synthesis_ref[...],
            x_ref[:, comp].reshape(LANES, LANES),
            precision=TOP_HARMONIC,
            preferred_element_type=jnp.float32,
        )
        for comp in range(3)
    ]
    elevation, eastward, northward = moments
    group = lax.axis_index("freq")
    depths = table_ref[ROW_DEPTHS, 3 + group // 8]
    depth = jnp.sum(jnp.where(iota((8, LANES), 0) == group % 8, depths, 0.0), axis=0, keepdims=True)
    column_depth = depth + 0.5 * jnp.tanh(elevation)
    magnitude = jnp.sqrt(eastward * eastward + northward * northward + SPEED_FLOOR)
    factor = FRICTION * magnitude / column_depth
    for comp, moving in enumerate((eastward, northward)):
        terms = jnp.dot(
            analysis_ref[...], factor * moving, precision=TOP_HARMONIC, preferred_element_type=jnp.float32
        )
        out_ref[:, comp] = terms.reshape(RANKS, 8, LANES)


def prepare_links(table_ref, shift, links_ref, index_ref):
    share = iota((8, LANES), 1) & (SHARE - 1)
    for half in range(2):
        rows = [table_ref[at, 3 + half] for at in range(RANKS)]
        spread = rows[0] + rows[1] + rows[2] + rows[3]
        values = rows[:12] + [
            spread + (ETA_DAMP - shift),
            spread + (rows[ROW_DAMPING] - shift),
            rows[4] + rows[5] + rows[6] + rows[7],
            rows[8] + rows[9] + rows[10] + rows[11],
        ]
        for i in range(8):
            for at, value in enumerate(values):
                links_ref[8 * half + i, at] = jnp.broadcast_to(value[i : i + 1], (8, LANES))
        for link in range(2):
            at = rows[ROW_LINKS + link].astype(jnp.int32)
            outside = jnp.logical_or(at < 0, at > RANKS - 1)
            lane = (at & (RANKS - 1)) * SHARE + share
            index = jnp.where(outside, lane + LANES, lane)
            for i in range(8):
                index_ref[8 * half + i, link] = jnp.broadcast_to(index[i : i + 1], (8, LANES))


def apply_operator(vectors, links_ref, index_ref):
    lane = iota((8, LANES), 1)
    first = lane < SHARE
    last = lane >= LANES - SHARE
    result = []
    for g in range(RANKS):
        here = vectors[g]
        before = vectors[g - 1] if g > 0 else [pltpu.roll(x, LANES - 2 * SHARE, 1) for x in here]
        after = vectors[g + 1] if g < RANKS - 1 else [pltpu.roll(x, 2 * SHARE, 1) for x in here]
        beside = []
        beside.append([pltpu.roll(jnp.where(last, p, x), SHARE, 1) for p, x in zip(before, here)])
        beside.append([pltpu.roll(jnp.where(first, n, x), LANES - SHARE, 1) for n, x in zip(after, here)])
        edges = [jnp.where(last, p, n) for p, n in zip(before, after)]
        for link in range(2):
            index = index_ref[g, link]
            outside = index >= LANES
            index = index & (LANES - 1)
            beside.append(
                [
                    jnp.where(
                        outside,
                        jnp.take_along_axis(e, index, axis=1, mode="promise_in_bounds"),
                        jnp.take_along_axis(x, index, axis=1, mode="promise_in_bounds"),
                    )
                    for e, x in zip(edges, here)
                ]
            )
        x_ele, x_east, x_north = here
        eta_sum, flow_sum, east_sum, north_sum = [links_ref[g, 12 + at] for at in range(4)]
        ele = eta_sum * x_ele - east_sum * x_east - north_sum * x_north
        east = flow_sum * x_east - east_sum * x_ele - CORIOLIS * x_north
        north = flow_sum * x_north - north_sum * x_ele + CORIOLIS * x_east
        for link in range(4):
            y_ele, y_east, y_north = beside[link]
            weight, to_east, to_north = [links_ref[g, at + link] for at in (0, 4, 8)]
            ele = ele - weight * y_ele + to_east * y_east + to_north * y_north
            east = east - weight * y_east + to_east * y_ele
            north = north - weight * y_north + to_north * y_ele
        result.append([ele, east, north])
    return result


def slot_rows(ref, pick):
    first = lax.axis_index("freq") * 4
    slot = iota((8, LANES), 0) & 3
    values = [pick(ref, first + s) for s in range(4)]
    return jnp.where(slot == 0, values[0], jnp.where(slot == 1, values[1], jnp.where(slot == 2, values[2], values[3])))


def angular_rows(harmonic_ref):
    return OMEGA_STEP * slot_rows(harmonic_ref, lambda ref, i: ref[i]).astype(jnp.float32)


def start_kernel(given_ref, table_ref, harmonic_ref, base_ref, links_ref, index_ref, shift_ref):
    shift = given_ref[0, 6, 1:2]
    for g in range(1, RANKS):
        shift = shift + given_ref[g, 6, 1:2]
    shift = jnp.broadcast_to(shift * (1.0 / RANKS), (8, LANES))
    shift_ref[...] = shift
    prepare_links(table_ref, shift, links_ref, index_ref)
    turn = angular_rows(harmonic_ref) * jnp.where(iota((8, LANES), 0) < 4, -1.0, 1.0)
    vectors = [[given_ref[g, comp] for comp in range(3)] for g in range(RANKS)]
    images = apply_operator(vectors, links_ref, index_ref)
    for g in range(RANKS):
        for comp in range(3):
            rest = shift * vectors[g][comp] + turn * pltpu.roll(vectors[g][comp], 4, 0)
            base_ref[g, comp] = given_ref[g, 3 + comp] - images[g][comp] - rest


def basis_kernel(base_ref, friction_ref, links_ref, index_ref, basis_ref, gram_ref):
    for g in range(RANKS):
        basis_ref[0, g, 0] = base_ref[g, 0]
        basis_ref[0, g, 1] = base_ref[g, 1] - friction_ref[g, 0]
        basis_ref[0, g, 2] = base_ref[g, 2] - friction_ref[g, 1]

    def power(m, _):
        vectors = [[basis_ref[m, g, comp] for comp in range(3)] for g in range(RANKS)]
        images = apply_operator(vectors, links_ref, index_ref)
        for g in range(RANKS):
            for comp in range(3):
                basis_ref[m + 1, g, comp] = images[g][comp]
        return 0

    lax.fori_loop(0, LMAX, power, 0)

    def products(g, sums):
        for comp in range(3):
            vectors = [basis_ref[m, g, comp] for m in range(COUNT)]
            turned = [None] + [pltpu.roll(v, 4, 0) for v in vectors[1:]]
            terms = [vectors[m] * vectors[n] for m, n in REAL_PAIRS]
            terms += [vectors[m] * turned[n] for m, n in IMAG_PAIRS]
            sums = tuple(a + b for a, b in zip(sums, terms))
        return sums

    entries = len(REAL_PAIRS) + len(IMAG_PAIRS)
    sums = lax.fori_loop(0, RANKS, products, tuple(jnp.zeros((8, LANES), jnp.float32) for _ in range(entries)))
    lane = iota((8, LANES), 1)
    gram = jnp.zeros((8, LANES), jnp.float32)
    for entry, value in enumerate(sums):
        gram = jnp.where(lane == entry, jnp.sum(value, axis=1, keepdims=True), gram)
    turned = pltpu.roll(gram, 4, 0)
    gram = jnp.where(lane < len(REAL_PAIRS), gram + turned, gram - turned)
    packed = jnp.where(lane < LANES // 2, gram, pltpu.roll(pltpu.roll(gram, LANES // 2, 1), 6, 0))[:2]
    for rank in range(RANKS):
        gram_ref[rank] = packed


def step_sizes(gram_ref, shift, harmonic_ref, counts_ref, sweep):
    gram = gram_ref[0]
    for rank in range(1, RANKS):
        gram = gram + gram_ref[rank]
    swapped = pltpu.roll(gram, LANES // 2, 1)
    gram = jnp.concatenate([gram, swapped, gram, swapped], axis=0)

    def entry(values, at):
        return jnp.broadcast_to(values[:, at : at + 1], (8, LANES))

    inner = {}
    for at, (m, n) in enumerate(REAL_PAIRS):
        inner[m, n] = (entry(gram, at), None)
    for at, (m, n) in enumerate(IMAG_PAIRS):
        inner[m, n] = (inner[m, n][0], entry(gram, len(REAL_PAIRS) + at))

    def mul(a, b):
        return (a[0] * b[0] - a[1] * b[1], a[0] * b[1] + a[1] * b[0])

    def add(a, b):
        return (a[0] + b[0], a[1] + b[1])

    def conj_mul(a, b):
        return (a[0] * b[0] + a[1] * b[1], a[0] * b[1] - a[1] * b[0])

    def gram_times(m, n, b):
        if m == n:
            g = inner[m, n][0]
            return (g * b[0], g * b[1])
        if m < n:
            return mul(inner[m, n], b)
        return conj_mul(inner[n, m], b)

    angular = angular_rows(harmonic_ref)
    counts = slot_rows(counts_ref, lambda ref, i: ref[sweep, i])
    zero = jnp.zeros((8, LANES), jnp.float32)
    residual = [(jnp.ones((8, LANES), jnp.float32), zero)]
    correction = [(zero, zero) for _ in range(LMAX)]
    for step in range(LMAX):
        image = []
        for m in range(step + 2):
            value = (zero, zero)
            if m <= step:
                r = residual[m]
                value = (shift * r[0] - angular * r[1], shift * r[1] + angular * r[0])
            if m > 0:
                value = add(value, residual[m - 1])
            image.append(value)
        upper = (zero, zero)
        lower = zero
        for m in range(step + 2):
            with_residual = (zero, zero)
            for n in range(step + 1):
                with_residual = add(with_residual, gram_times(m, n, residual[n]))
            upper = add(upper, conj_mul(image[m], with_residual))
            with_image = (zero, zero)
            for n in range(step + 2):
                with_image = add(with_image, gram_times(m, n, image[n]))
            lower = lower + image[m][0] * with_image[0] + image[m][1] * with_image[1]
        lower = lower + 1e-06
        active = jnp.where(step < counts, 1.0, 0.0)
        alpha = (active * upper[0] / lower, active * upper[1] / lower)
        for m in range(step + 1):
            correction[m] = add(correction[m], mul(alpha, residual[m]))
        residual = residual + [(zero, zero)]
        for m in range(step + 2):
            change = mul(alpha, image[m])
            residual[m] = (residual[m][0] - change[0], residual[m][1] - change[1])
    return correction, residual


def combine(coefs, vectors, sign):
    straight = coefs[0][0] * vectors[0]
    turned = coefs[0][1] * vectors[0]
    for (real, imag), vector in zip(coefs[1:], vectors[1:]):
        straight = straight + real * vector
        turned = turned + imag * vector
    return straight + sign * pltpu.roll(turned, 4, 0)


def update_kernel(sweep, gram_ref, fields_ref, basis_ref, friction_ref, shift_ref, harmonic_ref, counts_ref, *outs):
    correction, residual = step_sizes(gram_ref, shift_ref[...], harmonic_ref, counts_ref, sweep)
    sign = jnp.where(iota((8, LANES), 0) < 4, -1.0, 1.0)

    def update(g, _):
        for comp in range(3):
            vectors = [basis_ref[m, g, comp] for m in range(COUNT)]
            fields = fields_ref[g, comp] + combine(correction, vectors[:LMAX], sign)
            left = combine(residual, vectors, sign)
            if sweep == SWEEPS - 1:
                outs[0][g, comp] = fields
                outs[0][g, 3 + comp] = left
            else:
                outs[0][g, comp] = fields
                outs[1][g, comp] = left if comp == 0 else left + friction_ref[g, comp - 1]
        return 0

    lax.fori_loop(0, RANKS, update, 0)


def struct(*shape):
    return jax.ShapeDtypeStruct(shape, jnp.float32)


def call(kernel, out, specs, scratch=(), mebibytes=16, out_specs=None):
    outs = out if isinstance(out, list) else [out]
    result = pl.pallas_call(
        kernel,
        out_shape=outs,
        in_specs=specs,
        out_specs=out_specs or [VMEM] * len(outs),
        scratch_shapes=list(scratch),
        compiler_params=pltpu.CompilerParams(vmem_limit_bytes=mebibytes * 1024 * 1024),
    )
    return (lambda *args: result(*args)) if isinstance(out, list) else (lambda *args: result(*args)[0])


def exchange(values, axis):
    return lax.all_to_all(values, axis, split_axis=0, concat_axis=0, tiled=True)


def rows_of(x):
    return x.transpose(0, 2, 1, 3).reshape(4, 3, 2, RANKS, LANES).transpose(0, 1, 3, 2, 4).reshape(-1, LANES)


def fields_of(rows):
    return rows.reshape(4, 3, RANKS, 2, LANES).transpose(0, 3, 1, 2, 4).reshape(4, 2, 3, RANKS * LANES)


def body(
    harmonics, forcing, depths, damping, weights, couple_east, couple_north, connections, counts, harmonic_of_slot
):
    whole = pltpu.VMEM((384, LANES), jnp.float32)
    four = pltpu.VMEM((4, 2048), jnp.float32)
    line = pltpu.VMEM((1, 2048), jnp.float32)
    packed = call(
        pack_kernel,
        struct(RANKS, 7, 8, LANES),
        [HBM] * 7 + [SMEM],
        (
            whole,
            whole,
            four,
            four,
            four,
            line,
            line,
            pltpu.VMEM((RANKS, 1, 2048), jnp.float32),
            pltpu.VMEM((RANKS, 7, 8, LANES), jnp.float32),
            pltpu.SemaphoreType.DMA((7,)),
            pltpu.SemaphoreType.DMA((3,)),
        ),
        58,
        [HBM],
    )(
        rows_of(harmonics),
        rows_of(forcing),
        weights,
        couple_east,
        couple_north,
        damping.reshape(1, -1),
        depths.reshape(1, -1),
        connections.T,
    )
    given = exchange(packed, "node")
    table = exchange(call(forward_kernel, struct(RANKS, 5, 8, LANES), [VMEM])(given), "freq")

    slots = jnp.broadcast_to(harmonic_of_slot.reshape(RANKS, 1, 4), (RANKS, 2, 4)).reshape(1, LANES)
    cosines = np.cos(np.arange(SAMPLES) * (2.0 * math.pi / SAMPLES)).astype(np.float32).reshape(1, SAMPLES)

    synthesis, analysis = call(tables_kernel, [struct(SAMPLES, LANES), struct(LANES, SAMPLES)], [VMEM] * 2)(
        slots, cosines
    )

    def friction_of(received):
        terms = call(friction_kernel, struct(RANKS, 2, 8, LANES), [VMEM] * 4)(received, table, synthesis, analysis)
        return exchange(terms, "freq")

    base, links, index, shift = call(
        start_kernel,
        [
            struct(RANKS, 3, 8, LANES),
            struct(RANKS, 16, 8, LANES),
            jax.ShapeDtypeStruct((RANKS, 2, 8, LANES), jnp.int32),
            struct(8, LANES),
        ],
        [VMEM, VMEM, SMEM],
    )(given, table, harmonic_of_slot)
    fields = given
    friction = friction_of(table)
    for sweep in range(SWEEPS):
        basis, gram = call(
            basis_kernel, [struct(COUNT, RANKS, 3, 8, LANES), struct(RANKS, 2, LANES)], [VMEM] * 4
        )(base, friction, links, index)
        gram = exchange(gram, "node")
        if sweep < SWEEPS - 1:
            outs = [struct(RANKS, 3, 8, LANES), struct(RANKS, 3, 8, LANES)]
        else:
            outs = [struct(RANKS, 6, 8, LANES)]
        results = call(functools.partial(update_kernel, sweep), outs, [VMEM] * 5 + [SMEM] * 2)(
            gram, fields, basis, friction, shift, harmonic_of_slot, counts
        )
        if sweep < SWEEPS - 1:
            fields, base = results
            friction = friction_of(exchange(fields, "freq"))
    out = [struct(384, LANES)] * 2
    fields, residual = call(
        unpack_kernel, out, [VMEM], (whole, whole, pltpu.SemaphoreType.DMA((2,))), 16, [HBM] * 2
    )(exchange(results[0], "node"))
    return (fields_of(fields), fields_of(residual))


def solution(mesh):
    return jax.shard_map(
        body,
        mesh=mesh,
        in_specs=(
            P("freq", None, None, "node"),
            P("freq", None, None, "node"),
            P("node"),
            P("node"),
            P(None, "node"),
            P(None, "node"),
            P(None, "node"),
            P("node", None),
            P(),
            P(),
        ),
        out_specs=(P("freq", None, None, "node"), P("freq", None, None, "node")),
        check_vma=False,
    )
```

```python
import functools
import math

import jax
import jax.numpy as jnp
import numpy as np
from jax import lax
from jax.experimental import pallas as pl
from jax.experimental.pallas import tpu as pltpu
from jax.sharding import PartitionSpec as P

SAMPLES = 128
LMAX = 5
SWEEPS = 2

FRICTION = 2.0
CORIOLIS = 0.5
ETA_DAMP = 0.2
OMEGA_STEP = 0.05
SPEED_FLOOR = 0.01
TOP_HARMONIC = lax.Precision.HIGHEST

RANKS = 16
LANES = 128
SHARE = 8
COUNT = LMAX + 1
REAL_PAIRS = [(m, n) for m in range(COUNT) for n in range(m, COUNT)]
IMAG_PAIRS = [(m, n) for m in range(COUNT) for n in range(m + 1, COUNT)]
ROW_DAMPING, ROW_DEPTHS, ROW_LINKS = 12, 13, 14

VMEM = pl.BlockSpec(memory_space=pltpu.VMEM)
HBM = pl.BlockSpec(memory_space=pl.ANY)
SMEM = pl.BlockSpec(memory_space=pltpu.SMEM)


def iota(shape, axis):
    return lax.broadcasted_iota(jnp.int32, shape, axis)


def swap_blocks(rows):
    lane = iota((8, LANES), 1)
    rows = list(rows)
    for bit in range(4):
        step = SHARE << bit
        upper = (lane & step) != 0
        for i in range(RANKS):
            if i & (1 << bit):
                continue
            low, high = rows[i], rows[i | (1 << bit)]
            rows[i] = jnp.where(upper, pltpu.roll(high, step, 1), low)
            rows[i | (1 << bit)] = jnp.where(upper, high, pltpu.roll(low, LANES - step, 1))
    return rows


def pack_group(rows_of, out_ref, group):
    rows = [rows_of(b) for b in range(RANKS)]
    for rank, row in enumerate(swap_blocks(rows)):
        out_ref[rank, group] = row


def pack_kernel(
    fields_hbm,
    forcing_hbm,
    weights_hbm,
    east_hbm,
    north_hbm,
    damping_hbm,
    depths_hbm,
    links_ref,
    out_hbm,
    fields_ref,
    forcing_ref,
    weights_ref,
    east_ref,
    north_ref,
    damping_ref,
    depths_ref,
    rows_ref,
    out_ref,
    sems,
    out_sems,
):
    sources = (fields_hbm, forcing_hbm, weights_hbm, east_hbm, north_hbm, damping_hbm, depths_hbm)
    targets = (fields_ref, forcing_ref, weights_ref, east_ref, north_ref, damping_ref, depths_ref)
    copies = [pltpu.make_async_copy(a, b, sems.at[i]) for i, (a, b) in enumerate(zip(sources, targets))]
    for copy in copies:
        copy.start()
    first = lax.axis_index("node") * RANKS
    for link in range(2):
        for b in range(RANKS):
            local = (links_ref[2 + link, b] - first).astype(jnp.float32)
            at = ROW_LINKS + link
            rows_ref[at, :, LANES * b : LANES * (b + 1)] = jnp.full((1, LANES), local, jnp.float32)
    sent = []

    def send(index, group, count):
        part = pl.ds(group, count)
        copy = pltpu.make_async_copy(out_ref.at[:, part], out_hbm.at[:, part], out_sems.at[index])
        copy.start()
        sent.append(copy)

    for group in range(6):
        if group % 3 == 0:
            copies[group // 3].wait()
        source = (fields_ref, forcing_ref)[group // 3]

        def block(b):
            start = 32 * (group % 3) + 2 * b
            parts = [source[pl.ds(start + part, 4, stride=96), :] for part in range(2)]
            return jnp.concatenate(parts, axis=0)

        pack_group(block, out_ref, group)
        if group % 3 == 2:
            send(group // 3, group - 2, 3)
    for copy in copies[2:]:
        copy.wait()
    for kind, source in enumerate((weights_ref, east_ref, north_ref)):
        for link in range(4):
            rows_ref[4 * kind + link] = source[link : link + 1, :]
    rows_ref[ROW_DAMPING] = damping_ref[...]
    rows_ref[ROW_DEPTHS] = depths_ref[...]
    mine = lax.axis_index("freq")
    rows = [jnp.broadcast_to(rows_ref[mine, :, LANES * b : LANES * (b + 1)], (8, LANES)) for b in range(RANKS)]
    diagonal = jnp.sum(weights_ref[...], axis=0, keepdims=True) + (2.0 / 3.0) * damping_ref[...] + ETA_DAMP / 3.0
    mean = jnp.sum(diagonal, axis=1, keepdims=True) * (1.0 / diagonal.shape[1])
    top = iota((8, LANES), 0) == 0
    for rank, row in enumerate(swap_blocks(rows)):
        out_ref[rank, 6] = jnp.where(top, row, mean)
    send(2, 6, 1)
    for copy in sent:
        copy.wait()


def forward_kernel(given_ref, _, out_ref):
    for half in range(2):
        rows = jnp.concatenate([given_ref[8 * half + i, 6, 0:1] for i in range(8)], axis=0)
        for rank in range(RANKS):
            out_ref[rank, 3 + half] = rows
    for rank in range(RANKS):
        for comp in range(3):
            out_ref[rank, comp] = given_ref[rank, comp]


def unpack_kernel(x_ref, fields_hbm, residual_hbm, fields_ref, residual_ref, sems):
    copies = []
    for i, (target, out) in enumerate(((fields_ref, fields_hbm), (residual_ref, residual_hbm))):
        for comp in range(3):
            rows = swap_blocks([x_ref[rank, 3 * i + comp] for rank in range(RANKS)])
            for b, row in enumerate(rows):
                for part in range(2):
                    target[pl.ds(32 * comp + 2 * b + part, 4, stride=96), :] = row[4 * part : 4 * part + 4]
        copies.append(pltpu.make_async_copy(target, out, sems.at[i]))
        copies[-1].start()
    for copy in copies:
        copy.wait()


def tables_kernel(harmonic_ref, cosines_ref, synthesis_ref, analysis_ref):
    samples = iota((SAMPLES, LANES), 0)
    quarter = jnp.where((iota((SAMPLES, LANES), 1) & 4) != 0, SAMPLES // 4, 0)
    harmonic = jnp.broadcast_to(harmonic_ref[...], (SAMPLES, LANES))
    turn = (samples * harmonic + quarter) & (SAMPLES - 1)
    cosines = jnp.broadcast_to(cosines_ref[...], (SAMPLES, LANES))
    synthesis = jnp.take_along_axis(cosines, turn, axis=1, mode="promise_in_bounds")
    synthesis_ref[...] = synthesis
    analysis_ref[...] = (synthesis * jnp.where(harmonic == 0, 1.0 / SAMPLES, 2.0 / SAMPLES)).T


def friction_kernel(x_ref, table_ref, synthesis_ref, analysis_ref, out_ref):
    moments = [
        jnp.dot(
            synthesis_ref[...],
            x_ref[:, comp].reshape(LANES, LANES),
            precision=TOP_HARMONIC,
            preferred_element_type=jnp.float32,
        )
        for comp in range(3)
    ]
    elevation, eastward, northward = moments
    group = lax.axis_index("freq")
    depths = table_ref[ROW_DEPTHS, 3 + group // 8]
    depth = jnp.sum(jnp.where(iota((8, LANES), 0) == group % 8, depths, 0.0), axis=0, keepdims=True)
    column_depth = depth + 0.5 * jnp.tanh(elevation)
    magnitude = jnp.sqrt(eastward * eastward + northward * northward + SPEED_FLOOR)
    factor = FRICTION * magnitude / column_depth
    for comp, moving in enumerate((eastward, northward)):
        terms = jnp.dot(
            analysis_ref[...], factor * moving, precision=TOP_HARMONIC, preferred_element_type=jnp.float32
        )
        out_ref[:, comp] = terms.reshape(RANKS, 8, LANES)


def prepare_links(table_ref, shift, links_ref, index_ref):
    share = iota((8, LANES), 1) & (SHARE - 1)
    for half in range(2):
        rows = [table_ref[at, 3 + half] for at in range(RANKS)]
        spread = rows[0] + rows[1] + rows[2] + rows[3]
        values = rows[:12] + [
            spread + (ETA_DAMP - shift),
            spread + (rows[ROW_DAMPING] - shift),
            rows[4] + rows[5] + rows[6] + rows[7],
            rows[8] + rows[9] + rows[10] + rows[11],
        ]
        for i in range(8):
            for at, value in enumerate(values):
                links_ref[8 * half + i, at] = jnp.broadcast_to(value[i : i + 1], (8, LANES))
        for link in range(2):
            at = rows[ROW_LINKS + link].astype(jnp.int32)
            outside = jnp.logical_or(at < 0, at > RANKS - 1)
            lane = (at & (RANKS - 1)) * SHARE + share
            index = jnp.where(outside, lane + LANES, lane)
            for i in range(8):
                index_ref[8 * half + i, link] = jnp.broadcast_to(index[i : i + 1], (8, LANES))


def apply_operator(vectors, links_ref, index_ref):
    lane = iota((8, LANES), 1)
    first = lane < SHARE
    last = lane >= LANES - SHARE
    result = []
    for g in range(RANKS):
        here = vectors[g]
        before = vectors[g - 1] if g > 0 else [pltpu.roll(x, LANES - 2 * SHARE, 1) for x in here]
        after = vectors[g + 1] if g < RANKS - 1 else [pltpu.roll(x, 2 * SHARE, 1) for x in here]
        beside = []
        beside.append([pltpu.roll(jnp.where(last, p, x), SHARE, 1) for p, x in zip(before, here)])
        beside.append([pltpu.roll(jnp.where(first, n, x), LANES - SHARE, 1) for n, x in zip(after, here)])
        edges = [jnp.where(last, p, n) for p, n in zip(before, after)]
        for link in range(2):
            index = index_ref[g, link]
            outside = index >= LANES
            index = index & (LANES - 1)
            beside.append(
                [
                    jnp.where(
                        outside,
                        jnp.take_along_axis(e, index, axis=1, mode="promise_in_bounds"),
                        jnp.take_along_axis(x, index, axis=1, mode="promise_in_bounds"),
                    )
                    for e, x in zip(edges, here)
                ]
            )
        x_ele, x_east, x_north = here
        eta_sum, flow_sum, east_sum, north_sum = [links_ref[g, 12 + at] for at in range(4)]
        ele = eta_sum * x_ele - east_sum * x_east - north_sum * x_north
        east = flow_sum * x_east - east_sum * x_ele - CORIOLIS * x_north
        north = flow_sum * x_north - north_sum * x_ele + CORIOLIS * x_east
        for link in range(4):
            y_ele, y_east, y_north = beside[link]
            weight, to_east, to_north = [links_ref[g, at + link] for at in (0, 4, 8)]
            ele = ele - weight * y_ele + to_east * y_east + to_north * y_north
            east = east - weight * y_east + to_east * y_ele
            north = north - weight * y_north + to_north * y_ele
        result.append([ele, east, north])
    return result


def slot_rows(ref, pick):
    first = lax.axis_index("freq") * 4
    slot = iota((8, LANES), 0) & 3
    values = [pick(ref, first + s) for s in range(4)]
    return jnp.where(slot == 0, values[0], jnp.where(slot == 1, values[1], jnp.where(slot == 2, values[2], values[3])))


def angular_rows(harmonic_ref):
    return OMEGA_STEP * slot_rows(harmonic_ref, lambda ref, i: ref[i]).astype(jnp.float32)


def start_kernel(given_ref, table_ref, harmonic_ref, base_ref, links_ref, index_ref, shift_ref):
    shift = given_ref[0, 6, 1:2]
    for g in range(1, RANKS):
        shift = shift + given_ref[g, 6, 1:2]
    shift = jnp.broadcast_to(shift * (1.0 / RANKS), (8, LANES))
    shift_ref[...] = shift
    prepare_links(table_ref, shift, links_ref, index_ref)
    turn = angular_rows(harmonic_ref) * jnp.where(iota((8, LANES), 0) < 4, -1.0, 1.0)
    vectors = [[given_ref[g, comp] for comp in range(3)] for g in range(RANKS)]
    images = apply_operator(vectors, links_ref, index_ref)
    for g in range(RANKS):
        for comp in range(3):
            rest = shift * vectors[g][comp] + turn * pltpu.roll(vectors[g][comp], 4, 0)
            base_ref[g, comp] = given_ref[g, 3 + comp] - images[g][comp] - rest


def basis_kernel(base_ref, friction_ref, links_ref, index_ref, basis_ref, gram_ref, swap_ref):
    for g in range(RANKS):
        basis_ref[0, g, 0] = base_ref[g, 0]
        basis_ref[0, g, 1] = base_ref[g, 1] - friction_ref[g, 0]
        basis_ref[0, g, 2] = base_ref[g, 2] - friction_ref[g, 1]

    def power(m, _):
        vectors = [[basis_ref[m, g, comp] for comp in range(3)] for g in range(RANKS)]
        images = apply_operator(vectors, links_ref, index_ref)
        for g in range(RANKS):
            for comp in range(3):
                basis_ref[m + 1, g, comp] = images[g][comp]
                swap_ref[m, g, comp, pl.ds(0, 8, stride=2), :] = images[g][comp]
                swap_ref[m, g, comp, pl.ds(16, 8, stride=2), :] = images[g][comp]
        return 0

    lax.fori_loop(0, LMAX, power, 0)

    def products(g, sums):
        for comp in range(3):
            vectors = [basis_ref[m, g, comp] for m in range(COUNT)]
            turned = [None] + [swap_ref[m, g, comp, pl.ds(8, 8, stride=2), :] for m in range(LMAX)]
            terms = [vectors[m] * vectors[n] for m, n in REAL_PAIRS]
            terms += [vectors[m] * turned[n] for m, n in IMAG_PAIRS]
            sums = tuple(a + b for a, b in zip(sums, terms))
        return sums

    entries = len(REAL_PAIRS) + len(IMAG_PAIRS)
    sums = lax.fori_loop(0, RANKS, products, tuple(jnp.zeros((8, LANES), jnp.float32) for _ in range(entries)))
    lane = iota((8, LANES), 1)
    gram = jnp.zeros((8, LANES), jnp.float32)
    for entry, value in enumerate(sums):
        gram = jnp.where(lane == entry, jnp.sum(value, axis=1, keepdims=True), gram)
    turned = pltpu.roll(gram, 4, 0)
    gram = jnp.where(lane < len(REAL_PAIRS), gram + turned, gram - turned)
    packed = jnp.where(lane < LANES // 2, gram, pltpu.roll(pltpu.roll(gram, LANES // 2, 1), 6, 0))[:2]
    for rank in range(RANKS):
        gram_ref[rank] = packed


def step_sizes(gram_ref, shift, harmonic_ref, counts_ref, sweep):
    gram = gram_ref[0]
    for rank in range(1, RANKS):
        gram = gram + gram_ref[rank]
    swapped = pltpu.roll(gram, LANES // 2, 1)
    gram = jnp.concatenate([gram, swapped, gram, swapped], axis=0)

    def entry(values, at):
        return jnp.broadcast_to(values[:, at : at + 1], (8, LANES))

    inner = {}
    for at, (m, n) in enumerate(REAL_PAIRS):
        inner[m, n] = (entry(gram, at), None)
    for at, (m, n) in enumerate(IMAG_PAIRS):
        inner[m, n] = (inner[m, n][0], entry(gram, len(REAL_PAIRS) + at))

    def mul(a, b):
        return (a[0] * b[0] - a[1] * b[1], a[0] * b[1] + a[1] * b[0])

    def add(a, b):
        return (a[0] + b[0], a[1] + b[1])

    def conj_mul(a, b):
        return (a[0] * b[0] + a[1] * b[1], a[0] * b[1] - a[1] * b[0])

    def gram_times(m, n, b):
        if m == n:
            g = inner[m, n][0]
            return (g * b[0], g * b[1])
        if m < n:
            return mul(inner[m, n], b)
        return conj_mul(inner[n, m], b)

    angular = angular_rows(harmonic_ref)
    counts = slot_rows(counts_ref, lambda ref, i: ref[sweep, i])
    zero = jnp.zeros((8, LANES), jnp.float32)
    residual = [(jnp.ones((8, LANES), jnp.float32), zero)]
    correction = [(zero, zero) for _ in range(LMAX)]
    for step in range(LMAX):
        image = []
        for m in range(step + 2):
            value = (zero, zero)
            if m <= step:
                r = residual[m]
                value = (shift * r[0] - angular * r[1], shift * r[1] + angular * r[0])
            if m > 0:
                value = add(value, residual[m - 1])
            image.append(value)
        upper = (zero, zero)
        lower = zero
        for m in range(step + 2):
            with_residual = (zero, zero)
            for n in range(step + 1):
                with_residual = add(with_residual, gram_times(m, n, residual[n]))
            upper = add(upper, conj_mul(image[m], with_residual))
            with_image = (zero, zero)
            for n in range(step + 2):
                with_image = add(with_image, gram_times(m, n, image[n]))
            lower = lower + image[m][0] * with_image[0] + image[m][1] * with_image[1]
        lower = lower + 1e-06
        active = jnp.where(step < counts, 1.0, 0.0)
        alpha = (active * upper[0] / lower, active * upper[1] / lower)
        for m in range(step + 1):
            correction[m] = add(correction[m], mul(alpha, residual[m]))
        residual = residual + [(zero, zero)]
        for m in range(step + 2):
            change = mul(alpha, image[m])
            residual[m] = (residual[m][0] - change[0], residual[m][1] - change[1])
    return correction, residual


def combine(coefs, vectors, sign):
    straight = coefs[0][0] * vectors[0]
    turned = coefs[0][1] * vectors[0]
    for (real, imag), vector in zip(coefs[1:], vectors[1:]):
        straight = straight + real * vector
        turned = turned + imag * vector
    return straight + sign * pltpu.roll(turned, 4, 0)


def update_kernel(sweep, gram_ref, fields_ref, basis_ref, friction_ref, shift_ref, harmonic_ref, counts_ref, *outs):
    correction, residual = step_sizes(gram_ref, shift_ref[...], harmonic_ref, counts_ref, sweep)
    sign = jnp.where(iota((8, LANES), 0) < 4, -1.0, 1.0)

    def update(g, _):
        for comp in range(3):
            vectors = [basis_ref[m, g, comp] for m in range(COUNT)]
            fields = fields_ref[g, comp] + combine(correction, vectors[:LMAX], sign)
            left = combine(residual, vectors, sign)
            if sweep == SWEEPS - 1:
                outs[0][g, comp] = fields
                outs[0][g, 3 + comp] = left
            else:
                outs[0][g, comp] = fields
                outs[1][g, comp] = left if comp == 0 else left + friction_ref[g, comp - 1]
        return 0

    lax.fori_loop(0, RANKS, update, 0)


def struct(*shape):
    return jax.ShapeDtypeStruct(shape, jnp.float32)


def call(kernel, out, specs, scratch=(), mebibytes=16, out_specs=None):
    outs = out if isinstance(out, list) else [out]
    result = pl.pallas_call(
        kernel,
        out_shape=outs,
        in_specs=specs,
        out_specs=out_specs or [VMEM] * len(outs),
        scratch_shapes=list(scratch),
        compiler_params=pltpu.CompilerParams(vmem_limit_bytes=mebibytes * 1024 * 1024),
    )
    return (lambda *args: result(*args)) if isinstance(out, list) else (lambda *args: result(*args)[0])


def exchange(values, axis):
    return lax.all_to_all(values, axis, split_axis=0, concat_axis=0, tiled=True)


def rows_of(x):
    return x.transpose(0, 2, 1, 3).reshape(4, 3, 2, RANKS, LANES).transpose(0, 1, 3, 2, 4).reshape(-1, LANES)


def fields_of(rows):
    return rows.reshape(4, 3, RANKS, 2, LANES).transpose(0, 3, 1, 2, 4).reshape(4, 2, 3, RANKS * LANES)


def body(
    harmonics, forcing, depths, damping, weights, couple_east, couple_north, connections, counts, harmonic_of_slot
):
    whole = pltpu.VMEM((384, LANES), jnp.float32)
    four = pltpu.VMEM((4, 2048), jnp.float32)
    line = pltpu.VMEM((1, 2048), jnp.float32)
    packed = call(
        pack_kernel,
        struct(RANKS, 7, 8, LANES),
        [HBM] * 7 + [SMEM],
        (
            whole,
            whole,
            four,
            four,
            four,
            line,
            line,
            pltpu.VMEM((RANKS, 1, 2048), jnp.float32),
            pltpu.VMEM((RANKS, 7, 8, LANES), jnp.float32),
            pltpu.SemaphoreType.DMA((7,)),
            pltpu.SemaphoreType.DMA((3,)),
        ),
        58,
        [HBM],
    )(
        rows_of(harmonics),
        rows_of(forcing),
        weights,
        couple_east,
        couple_north,
        damping.reshape(1, -1),
        depths.reshape(1, -1),
        connections.T,
    )
    given = exchange(packed, "node")
    slots = jnp.broadcast_to(harmonic_of_slot.reshape(RANKS, 1, 4), (RANKS, 2, 4)).reshape(1, LANES)
    cosines = np.cos(np.arange(SAMPLES) * (2.0 * math.pi / SAMPLES)).astype(np.float32).reshape(1, SAMPLES)

    synthesis, analysis = call(tables_kernel, [struct(SAMPLES, LANES), struct(LANES, SAMPLES)], [VMEM] * 2)(
        slots, cosines
    )
    table = exchange(call(forward_kernel, struct(RANKS, 5, 8, LANES), [VMEM, HBM])(given, analysis), "freq")

    def friction_of(received):
        terms = call(friction_kernel, struct(RANKS, 2, 8, LANES), [VMEM] * 4)(received, table, synthesis, analysis)
        return exchange(terms, "freq")

    base, links, index, shift = call(
        start_kernel,
        [
            struct(RANKS, 3, 8, LANES),
            struct(RANKS, 16, 8, LANES),
            jax.ShapeDtypeStruct((RANKS, 2, 8, LANES), jnp.int32),
            struct(8, LANES),
        ],
        [VMEM, VMEM, SMEM],
    )(given, table, harmonic_of_slot)
    fields = given
    friction = friction_of(table)
    for sweep in range(SWEEPS):
        basis, gram = call(
            basis_kernel,
            [struct(COUNT, RANKS, 3, 8, LANES), struct(RANKS, 2, LANES)],
            [VMEM] * 4,
            (pltpu.VMEM((LMAX, RANKS, 3, 32, LANES), jnp.float32),),
        )(base, friction, links, index)
        gram = exchange(gram, "node")
        if sweep < SWEEPS - 1:
            outs = [struct(RANKS, 3, 8, LANES), struct(RANKS, 3, 8, LANES)]
        else:
            outs = [struct(RANKS, 6, 8, LANES)]
        results = call(functools.partial(update_kernel, sweep), outs, [VMEM] * 5 + [SMEM] * 2)(
            gram, fields, basis, friction, shift, harmonic_of_slot, counts
        )
        if sweep < SWEEPS - 1:
            fields, base = results
            friction = friction_of(exchange(fields, "freq"))
    out = [struct(384, LANES)] * 2
    fields, residual = call(
        unpack_kernel, out, [VMEM], (whole, whole, pltpu.SemaphoreType.DMA((2,))), 16, [HBM] * 2
    )(exchange(results[0], "node"))
    return (fields_of(fields), fields_of(residual))


def solution(mesh):
    return jax.shard_map(
        body,
        mesh=mesh,
        in_specs=(
            P("freq", None, None, "node"),
            P("freq", None, None, "node"),
            P("node"),
            P("node"),
            P(None, "node"),
            P(None, "node"),
            P(None, "node"),
            P("node", None),
            P(),
            P(),
        ),
        out_specs=(P("freq", None, None, "node"), P("freq", None, None, "node")),
        check_vma=False,
    )
```

```python
import functools
import math

import jax
import jax.numpy as jnp
import numpy as np
from jax import lax
from jax.experimental import pallas as pl
from jax.experimental.pallas import tpu as pltpu
from jax.sharding import PartitionSpec as P

SAMPLES = 128
LMAX = 5
SWEEPS = 2

FRICTION = 2.0
CORIOLIS = 0.5
ETA_DAMP = 0.2
OMEGA_STEP = 0.05
SPEED_FLOOR = 0.01
TOP_HARMONIC = lax.Precision.HIGHEST

RANKS = 16
LANES = 128
SHARE = 8
COUNT = LMAX + 1
REAL_PAIRS = [(m, n) for m in range(COUNT) for n in range(m, COUNT)]
IMAG_PAIRS = [(m, n) for m in range(COUNT) for n in range(m + 1, COUNT)]
ROW_DAMPING, ROW_DEPTHS, ROW_LINKS = 12, 13, 14

VMEM = pl.BlockSpec(memory_space=pltpu.VMEM)
HBM = pl.BlockSpec(memory_space=pl.ANY)
SMEM = pl.BlockSpec(memory_space=pltpu.SMEM)


def iota(shape, axis):
    return lax.broadcasted_iota(jnp.int32, shape, axis)


def swap_blocks(rows):
    lane = iota((8, LANES), 1)
    rows = list(rows)
    for bit in range(4):
        step = SHARE << bit
        upper = (lane & step) != 0
        for i in range(RANKS):
            if i & (1 << bit):
                continue
            low, high = rows[i], rows[i | (1 << bit)]
            rows[i] = jnp.where(upper, pltpu.roll(high, step, 1), low)
            rows[i | (1 << bit)] = jnp.where(upper, high, pltpu.roll(low, LANES - step, 1))
    return rows


def pack_group(rows_of, out_ref, group):
    rows = [rows_of(b) for b in range(RANKS)]
    for rank, row in enumerate(swap_blocks(rows)):
        out_ref[rank, group] = row


def pack_kernel(
    fields_hbm,
    forcing_hbm,
    weights_hbm,
    east_hbm,
    north_hbm,
    damping_hbm,
    depths_hbm,
    links_ref,
    out_hbm,
    fields_ref,
    forcing_ref,
    weights_ref,
    east_ref,
    north_ref,
    damping_ref,
    depths_ref,
    rows_ref,
    out_ref,
    sems,
    out_sems,
):
    sources = (fields_hbm, forcing_hbm, weights_hbm, east_hbm, north_hbm, damping_hbm, depths_hbm)
    targets = (fields_ref, forcing_ref, weights_ref, east_ref, north_ref, damping_ref, depths_ref)
    copies = [pltpu.make_async_copy(a, b, sems.at[i]) for i, (a, b) in enumerate(zip(sources, targets))]
    for copy in copies:
        copy.start()
    first = lax.axis_index("node") * RANKS
    for link in range(2):
        for b in range(RANKS):
            local = (links_ref[2 + link, b] - first).astype(jnp.float32)
            at = ROW_LINKS + link
            rows_ref[at, :, LANES * b : LANES * (b + 1)] = jnp.full((1, LANES), local, jnp.float32)
    sent = []

    def send(index, group, count):
        part = pl.ds(group, count)
        copy = pltpu.make_async_copy(out_ref.at[:, part], out_hbm.at[:, part], out_sems.at[index])
        copy.start()
        sent.append(copy)

    for group in range(6):
        if group % 3 == 0:
            copies[group // 3].wait()
        source = (fields_ref, forcing_ref)[group // 3]

        def block(b):
            start = 32 * (group % 3) + 2 * b
            parts = [source[pl.ds(start + part, 4, stride=96), :] for part in range(2)]
            return jnp.concatenate(parts, axis=0)

        pack_group(block, out_ref, group)
        if group % 3 == 2:
            send(group // 3, group - 2, 3)
    for copy in copies[2:]:
        copy.wait()
    for kind, source in enumerate((weights_ref, east_ref, north_ref)):
        for link in range(4):
            rows_ref[4 * kind + link] = source[link : link + 1, :]
    rows_ref[ROW_DAMPING] = damping_ref[...]
    rows_ref[ROW_DEPTHS] = depths_ref[...]
    mine = lax.axis_index("freq")
    rows = [jnp.broadcast_to(rows_ref[mine, :, LANES * b : LANES * (b + 1)], (8, LANES)) for b in range(RANKS)]
    diagonal = jnp.sum(weights_ref[...], axis=0, keepdims=True) + (2.0 / 3.0) * damping_ref[...] + ETA_DAMP / 3.0
    mean = jnp.sum(diagonal, axis=1, keepdims=True) * (1.0 / diagonal.shape[1])
    top = iota((8, LANES), 0) == 0
    for rank, row in enumerate(swap_blocks(rows)):
        out_ref[rank, 6] = jnp.where(top, row, mean)
    send(2, 6, 1)
    for copy in sent:
        copy.wait()


def forward_kernel(given_ref, _, out_ref):
    for half in range(2):
        rows = jnp.concatenate([given_ref[8 * half + i, 6, 0:1] for i in range(8)], axis=0)
        for rank in range(RANKS):
            out_ref[rank, 3 + half] = rows
    for rank in range(RANKS):
        for comp in range(3):
            out_ref[rank, comp] = given_ref[rank, comp]


def unpack_kernel(x_ref, fields_hbm, residual_hbm, fields_ref, residual_ref, sems):
    copies = []
    for i, (target, out) in enumerate(((fields_ref, fields_hbm), (residual_ref, residual_hbm))):
        for comp in range(3):
            rows = swap_blocks([x_ref[rank, 3 * i + comp] for rank in range(RANKS)])
            for b, row in enumerate(rows):
                for part in range(2):
                    target[pl.ds(32 * comp + 2 * b + part, 4, stride=96), :] = row[4 * part : 4 * part + 4]
        copies.append(pltpu.make_async_copy(target, out, sems.at[i]))
        copies[-1].start()
    for copy in copies:
        copy.wait()


def tables_kernel(harmonic_ref, cosines_ref, synthesis_ref, analysis_ref):
    samples = iota((SAMPLES, LANES), 0)
    quarter = jnp.where((iota((SAMPLES, LANES), 1) & 4) != 0, SAMPLES // 4, 0)
    harmonic = jnp.broadcast_to(harmonic_ref[...], (SAMPLES, LANES))
    turn = (samples * harmonic + quarter) & (SAMPLES - 1)
    cosines = jnp.broadcast_to(cosines_ref[...], (SAMPLES, LANES))
    synthesis = jnp.take_along_axis(cosines, turn, axis=1, mode="promise_in_bounds")
    synthesis_ref[...] = synthesis
    analysis_ref[...] = (synthesis * jnp.where(harmonic == 0, 1.0 / SAMPLES, 2.0 / SAMPLES)).T


def friction_kernel(x_ref, table_ref, synthesis_ref, analysis_ref, out_ref):
    moments = [
        jnp.dot(
            synthesis_ref[...],
            x_ref[:, comp].reshape(LANES, LANES),
            precision=TOP_HARMONIC,
            preferred_element_type=jnp.float32,
        )
        for comp in range(3)
    ]
    elevation, eastward, northward = moments
    group = lax.axis_index("freq")
    depths = table_ref[ROW_DEPTHS, 3 + group // 8]
    depth = jnp.sum(jnp.where(iota((8, LANES), 0) == group % 8, depths, 0.0), axis=0, keepdims=True)
    column_depth = depth + 0.5 * jnp.tanh(elevation)
    magnitude = jnp.sqrt(eastward * eastward + northward * northward + SPEED_FLOOR)
    factor = FRICTION * magnitude / column_depth
    for comp, moving in enumerate((eastward, northward)):
        terms = jnp.dot(
            analysis_ref[...], factor * moving, precision=TOP_HARMONIC, preferred_element_type=jnp.float32
        )
        out_ref[:, comp] = terms.reshape(RANKS, 8, LANES)


def prepare_links(table_ref, shift, links_ref, index_ref):
    share = iota((8, LANES), 1) & (SHARE - 1)
    for half in range(2):
        rows = [table_ref[at, 3 + half] for at in range(RANKS)]
        spread = rows[0] + rows[1] + rows[2] + rows[3]
        values = rows[:12] + [
            spread + (ETA_DAMP - shift),
            spread + (rows[ROW_DAMPING] - shift),
            rows[4] + rows[5] + rows[6] + rows[7],
            rows[8] + rows[9] + rows[10] + rows[11],
        ]
        for i in range(8):
            for at, value in enumerate(values):
                links_ref[8 * half + i, at] = jnp.broadcast_to(value[i : i + 1], (8, LANES))
        for link in range(2):
            at = rows[ROW_LINKS + link].astype(jnp.int32)
            lane = (at & (RANKS - 1)) * SHARE + share
            index = jnp.where(at < 0, lane + LANES, jnp.where(at > RANKS - 1, lane + 2 * LANES, lane))
            for i in range(8):
                index_ref[8 * half + i, link] = jnp.broadcast_to(index[i : i + 1], (8, LANES))


def make_moves(moves_ref):
    source, lane = iota((LANES, LANES), 0), iota((LANES, LANES), 1)
    share = lane & (SHARE - 1)
    for i, wanted in enumerate((share + (LANES - SHARE), share, lane - SHARE, lane + SHARE)):
        moves_ref[i] = jnp.where(source == wanted, 1.0, 0.0)


def move(vectors, moves_ref, moved_ref):
    rows = vectors.reshape(RANKS * 3 * 8, LANES)
    for i in range(4):
        result = jnp.dot(rows, moves_ref[i], precision=TOP_HARMONIC, preferred_element_type=jnp.float32)
        moved_ref[i] = result.reshape(RANKS, 3, 8, LANES)


def apply_operator(vectors, moved_ref, links_ref, index_ref):
    lane = iota((8, LANES), 1)
    first = lane < SHARE
    last = lane >= LANES - SHARE
    result = []
    for g in range(RANKS):
        here = vectors[g]
        on = [moved_ref[2, g, comp] for comp in range(3)]
        back = [moved_ref[3, g, comp] for comp in range(3)]
        before = [moved_ref[0, g - 1, comp] for comp in range(3)] if g > 0 else back
        after = [moved_ref[1, g + 1, comp] for comp in range(3)] if g < RANKS - 1 else on
        beside = []
        beside.append([jnp.where(first, p, x) for p, x in zip(before, on)])
        beside.append([jnp.where(last, n, x) for n, x in zip(after, back)])
        for link in range(2):
            index = index_ref[g, link]
            outside, following = index >= LANES, index >= 2 * LANES
            index = index & (LANES - 1)
            beside.append(
                [
                    jnp.where(
                        outside,
                        jnp.where(following, n, p),
                        jnp.take_along_axis(x, index, axis=1, mode="promise_in_bounds"),
                    )
                    for p, n, x in zip(before, after, here)
                ]
            )
        x_ele, x_east, x_north = here
        eta_sum, flow_sum, east_sum, north_sum = [links_ref[g, 12 + at] for at in range(4)]
        ele = eta_sum * x_ele - east_sum * x_east - north_sum * x_north
        east = flow_sum * x_east - east_sum * x_ele - CORIOLIS * x_north
        north = flow_sum * x_north - north_sum * x_ele + CORIOLIS * x_east
        for link in range(4):
            y_ele, y_east, y_north = beside[link]
            weight, to_east, to_north = [links_ref[g, at + link] for at in (0, 4, 8)]
            ele = ele - weight * y_ele + to_east * y_east + to_north * y_north
            east = east - weight * y_east + to_east * y_ele
            north = north - weight * y_north + to_north * y_ele
        result.append([ele, east, north])
    return result


def slot_rows(ref, pick):
    first = lax.axis_index("freq") * 4
    slot = iota((8, LANES), 0) & 3
    values = [pick(ref, first + s) for s in range(4)]
    return jnp.where(slot == 0, values[0], jnp.where(slot == 1, values[1], jnp.where(slot == 2, values[2], values[3])))


def angular_rows(harmonic_ref):
    return OMEGA_STEP * slot_rows(harmonic_ref, lambda ref, i: ref[i]).astype(jnp.float32)


def start_kernel(given_ref, table_ref, harmonic_ref, base_ref, links_ref, index_ref, shift_ref, moves_ref, moved_ref):
    shift = given_ref[0, 6, 1:2]
    for g in range(1, RANKS):
        shift = shift + given_ref[g, 6, 1:2]
    shift = jnp.broadcast_to(shift * (1.0 / RANKS), (8, LANES))
    shift_ref[...] = shift
    prepare_links(table_ref, shift, links_ref, index_ref)
    turn = angular_rows(harmonic_ref) * jnp.where(iota((8, LANES), 0) < 4, -1.0, 1.0)
    vectors = [[given_ref[g, comp] for comp in range(3)] for g in range(RANKS)]
    make_moves(moves_ref)
    move(given_ref[:, :3], moves_ref, moved_ref)
    images = apply_operator(vectors, moved_ref, links_ref, index_ref)
    for g in range(RANKS):
        for comp in range(3):
            rest = shift * vectors[g][comp] + turn * pltpu.roll(vectors[g][comp], 4, 0)
            base_ref[g, comp] = given_ref[g, 3 + comp] - images[g][comp] - rest


def basis_kernel(base_ref, friction_ref, links_ref, index_ref, basis_ref, gram_ref, swap_ref, moves_ref, moved_ref):
    make_moves(moves_ref)
    for g in range(RANKS):
        basis_ref[0, g, 0] = base_ref[g, 0]
        basis_ref[0, g, 1] = base_ref[g, 1] - friction_ref[g, 0]
        basis_ref[0, g, 2] = base_ref[g, 2] - friction_ref[g, 1]

    def power(m, _):
        vectors = [[basis_ref[m, g, comp] for comp in range(3)] for g in range(RANKS)]
        move(basis_ref[m], moves_ref, moved_ref)
        images = apply_operator(vectors, moved_ref, links_ref, index_ref)
        for g in range(RANKS):
            for comp in range(3):
                basis_ref[m + 1, g, comp] = images[g][comp]
                swap_ref[m, g, comp, pl.ds(0, 8, stride=2), :] = images[g][comp]
                swap_ref[m, g, comp, pl.ds(16, 8, stride=2), :] = images[g][comp]
        return 0

    lax.fori_loop(0, LMAX, power, 0)

    def products(g, sums):
        for comp in range(3):
            vectors = [basis_ref[m, g, comp] for m in range(COUNT)]
            turned = [None] + [swap_ref[m, g, comp, pl.ds(8, 8, stride=2), :] for m in range(LMAX)]
            terms = [vectors[m] * vectors[n] for m, n in REAL_PAIRS]
            terms += [vectors[m] * turned[n] for m, n in IMAG_PAIRS]
            sums = tuple(a + b for a, b in zip(sums, terms))
        return sums

    entries = len(REAL_PAIRS) + len(IMAG_PAIRS)
    sums = lax.fori_loop(0, RANKS, products, tuple(jnp.zeros((8, LANES), jnp.float32) for _ in range(entries)))
    lane = iota((8, LANES), 1)
    gram = jnp.zeros((8, LANES), jnp.float32)
    for entry, value in enumerate(sums):
        gram = jnp.where(lane == entry, jnp.sum(value, axis=1, keepdims=True), gram)
    turned = pltpu.roll(gram, 4, 0)
    gram = jnp.where(lane < len(REAL_PAIRS), gram + turned, gram - turned)
    packed = jnp.where(lane < LANES // 2, gram, pltpu.roll(pltpu.roll(gram, LANES // 2, 1), 6, 0))[:2]
    for rank in range(RANKS):
        gram_ref[rank] = packed


def step_sizes(gram_ref, shift, harmonic_ref, counts_ref, sweep):
    gram = gram_ref[0]
    for rank in range(1, RANKS):
        gram = gram + gram_ref[rank]
    swapped = pltpu.roll(gram, LANES // 2, 1)
    gram = jnp.concatenate([gram, swapped, gram, swapped], axis=0)

    def entry(values, at):
        return jnp.broadcast_to(values[:, at : at + 1], (8, LANES))

    inner = {}
    for at, (m, n) in enumerate(REAL_PAIRS):
        inner[m, n] = (entry(gram, at), None)
    for at, (m, n) in enumerate(IMAG_PAIRS):
        inner[m, n] = (inner[m, n][0], entry(gram, len(REAL_PAIRS) + at))

    def mul(a, b):
        return (a[0] * b[0] - a[1] * b[1], a[0] * b[1] + a[1] * b[0])

    def add(a, b):
        return (a[0] + b[0], a[1] + b[1])

    def conj_mul(a, b):
        return (a[0] * b[0] + a[1] * b[1], a[0] * b[1] - a[1] * b[0])

    def gram_times(m, n, b):
        if m == n:
            g = inner[m, n][0]
            return (g * b[0], g * b[1])
        if m < n:
            return mul(inner[m, n], b)
        return conj_mul(inner[n, m], b)

    angular = angular_rows(harmonic_ref)
    counts = slot_rows(counts_ref, lambda ref, i: ref[sweep, i])
    zero = jnp.zeros((8, LANES), jnp.float32)
    residual = [(jnp.ones((8, LANES), jnp.float32), zero)]
    correction = [(zero, zero) for _ in range(LMAX)]
    for step in range(LMAX):
        image = []
        for m in range(step + 2):
            value = (zero, zero)
            if m <= step:
                r = residual[m]
                value = (shift * r[0] - angular * r[1], shift * r[1] + angular * r[0])
            if m > 0:
                value = add(value, residual[m - 1])
            image.append(value)
        upper = (zero, zero)
        lower = zero
        for m in range(step + 2):
            with_residual = (zero, zero)
            for n in range(step + 1):
                with_residual = add(with_residual, gram_times(m, n, residual[n]))
            upper = add(upper, conj_mul(image[m], with_residual))
            with_image = (zero, zero)
            for n in range(step + 2):
                with_image = add(with_image, gram_times(m, n, image[n]))
            lower = lower + image[m][0] * with_image[0] + image[m][1] * with_image[1]
        lower = lower + 1e-06
        active = jnp.where(step < counts, 1.0, 0.0)
        alpha = (active * upper[0] / lower, active * upper[1] / lower)
        for m in range(step + 1):
            correction[m] = add(correction[m], mul(alpha, residual[m]))
        residual = residual + [(zero, zero)]
        for m in range(step + 2):
            change = mul(alpha, image[m])
            residual[m] = (residual[m][0] - change[0], residual[m][1] - change[1])
    return correction, residual


def combine(coefs, vectors, sign):
    straight = coefs[0][0] * vectors[0]
    turned = coefs[0][1] * vectors[0]
    for (real, imag), vector in zip(coefs[1:], vectors[1:]):
        straight = straight + real * vector
        turned = turned + imag * vector
    return straight + sign * pltpu.roll(turned, 4, 0)


def update_kernel(sweep, gram_ref, fields_ref, basis_ref, friction_ref, shift_ref, harmonic_ref, counts_ref, *outs):
    correction, residual = step_sizes(gram_ref, shift_ref[...], harmonic_ref, counts_ref, sweep)
    sign = jnp.where(iota((8, LANES), 0) < 4, -1.0, 1.0)

    def update(g, _):
        for comp in range(3):
            vectors = [basis_ref[m, g, comp] for m in range(COUNT)]
            fields = fields_ref[g, comp] + combine(correction, vectors[:LMAX], sign)
            left = combine(residual, vectors, sign)
            if sweep == SWEEPS - 1:
                outs[0][g, comp] = fields
                outs[0][g, 3 + comp] = left
            else:
                outs[0][g, comp] = fields
                outs[1][g, comp] = left if comp == 0 else left + friction_ref[g, comp - 1]
        return 0

    lax.fori_loop(0, RANKS, update, 0)


def struct(*shape):
    return jax.ShapeDtypeStruct(shape, jnp.float32)


def call(kernel, out, specs, scratch=(), mebibytes=16, out_specs=None):
    outs = out if isinstance(out, list) else [out]
    result = pl.pallas_call(
        kernel,
        out_shape=outs,
        in_specs=specs,
        out_specs=out_specs or [VMEM] * len(outs),
        scratch_shapes=list(scratch),
        compiler_params=pltpu.CompilerParams(vmem_limit_bytes=mebibytes * 1024 * 1024),
    )
    return (lambda *args: result(*args)) if isinstance(out, list) else (lambda *args: result(*args)[0])


def exchange(values, axis):
    return lax.all_to_all(values, axis, split_axis=0, concat_axis=0, tiled=True)


def rows_of(x):
    return x.transpose(0, 2, 1, 3).reshape(4, 3, 2, RANKS, LANES).transpose(0, 1, 3, 2, 4).reshape(-1, LANES)


def fields_of(rows):
    return rows.reshape(4, 3, RANKS, 2, LANES).transpose(0, 3, 1, 2, 4).reshape(4, 2, 3, RANKS * LANES)


def body(
    harmonics, forcing, depths, damping, weights, couple_east, couple_north, connections, counts, harmonic_of_slot
):
    whole = pltpu.VMEM((384, LANES), jnp.float32)
    four = pltpu.VMEM((4, 2048), jnp.float32)
    line = pltpu.VMEM((1, 2048), jnp.float32)
    moving = (pltpu.VMEM((4, LANES, LANES), jnp.float32), pltpu.VMEM((4, RANKS, 3, 8, LANES), jnp.float32))
    packed = call(
        pack_kernel,
        struct(RANKS, 7, 8, LANES),
        [HBM] * 7 + [SMEM],
        (
            whole,
            whole,
            four,
            four,
            four,
            line,
            line,
            pltpu.VMEM((RANKS, 1, 2048), jnp.float32),
            pltpu.VMEM((RANKS, 7, 8, LANES), jnp.float32),
            pltpu.SemaphoreType.DMA((7,)),
            pltpu.SemaphoreType.DMA((3,)),
        ),
        58,
        [HBM],
    )(
        rows_of(harmonics),
        rows_of(forcing),
        weights,
        couple_east,
        couple_north,
        damping.reshape(1, -1),
        depths.reshape(1, -1),
        connections.T,
    )
    given = exchange(packed, "node")
    slots = jnp.broadcast_to(harmonic_of_slot.reshape(RANKS, 1, 4), (RANKS, 2, 4)).reshape(1, LANES)
    cosines = np.cos(np.arange(SAMPLES) * (2.0 * math.pi / SAMPLES)).astype(np.float32).reshape(1, SAMPLES)

    synthesis, analysis = call(tables_kernel, [struct(SAMPLES, LANES), struct(LANES, SAMPLES)], [VMEM] * 2)(
        slots, cosines
    )
    table = exchange(call(forward_kernel, struct(RANKS, 5, 8, LANES), [VMEM, HBM])(given, analysis), "freq")

    def friction_of(received):
        terms = call(friction_kernel, struct(RANKS, 2, 8, LANES), [VMEM] * 4)(received, table, synthesis, analysis)
        return exchange(terms, "freq")

    base, links, index, shift = call(
        start_kernel,
        [
            struct(RANKS, 3, 8, LANES),
            struct(RANKS, 16, 8, LANES),
            jax.ShapeDtypeStruct((RANKS, 2, 8, LANES), jnp.int32),
            struct(8, LANES),
        ],
        [VMEM, VMEM, SMEM],
        moving,
    )(given, table, harmonic_of_slot)
    fields = given
    friction = friction_of(table)
    for sweep in range(SWEEPS):
        basis, gram = call(
            basis_kernel,
            [struct(COUNT, RANKS, 3, 8, LANES), struct(RANKS, 2, LANES)],
            [VMEM] * 4,
            (pltpu.VMEM((LMAX, RANKS, 3, 32, LANES), jnp.float32), *moving),
        )(base, friction, links, index)
        gram = exchange(gram, "node")
        if sweep < SWEEPS - 1:
            outs = [struct(RANKS, 3, 8, LANES), struct(RANKS, 3, 8, LANES)]
        else:
            outs = [struct(RANKS, 6, 8, LANES)]
        results = call(functools.partial(update_kernel, sweep), outs, [VMEM] * 5 + [SMEM] * 2)(
            gram, fields, basis, friction, shift, harmonic_of_slot, counts
        )
        if sweep < SWEEPS - 1:
            fields, base = results
            friction = friction_of(exchange(fields, "freq"))
    out = [struct(384, LANES)] * 2
    fields, residual = call(
        unpack_kernel, out, [VMEM], (whole, whole, pltpu.SemaphoreType.DMA((2,))), 16, [HBM] * 2
    )(exchange(results[0], "node"))
    return (fields_of(fields), fields_of(residual))


def solution(mesh):
    return jax.shard_map(
        body,
        mesh=mesh,
        in_specs=(
            P("freq", None, None, "node"),
            P("freq", None, None, "node"),
            P("node"),
            P("node"),
            P(None, "node"),
            P(None, "node"),
            P(None, "node"),
            P("node", None),
            P(),
            P(),
        ),
        out_specs=(P("freq", None, None, "node"), P("freq", None, None, "node")),
        check_vma=False,
    )
```

```python
import functools
import math

import jax
import jax.numpy as jnp
import numpy as np
from jax import lax
from jax.experimental import pallas as pl
from jax.experimental.pallas import tpu as pltpu
from jax.sharding import PartitionSpec as P

SAMPLES = 128
LMAX = 5
SWEEPS = 2

FRICTION = 2.0
CORIOLIS = 0.5
ETA_DAMP = 0.2
OMEGA_STEP = 0.05
SPEED_FLOOR = 0.01
TOP_HARMONIC = lax.Precision.HIGHEST

RANKS = 16
LANES = 128
SHARE = 8
COUNT = LMAX + 1
REAL_PAIRS = [(m, n) for m in range(COUNT) for n in range(m, COUNT)]
IMAG_PAIRS = [(m, n) for m in range(COUNT) for n in range(m + 1, COUNT)]
ROW_DAMPING, ROW_DEPTHS, ROW_LINKS = 12, 13, 14

VMEM = pl.BlockSpec(memory_space=pltpu.VMEM)
HBM = pl.BlockSpec(memory_space=pl.ANY)
SMEM = pl.BlockSpec(memory_space=pltpu.SMEM)


def iota(shape, axis):
    return lax.broadcasted_iota(jnp.int32, shape, axis)


def swap_blocks(rows):
    lane = iota((8, LANES), 1)
    rows = list(rows)
    for bit in range(4):
        step = SHARE << bit
        upper = (lane & step) != 0
        for i in range(RANKS):
            if i & (1 << bit):
                continue
            low, high = rows[i], rows[i | (1 << bit)]
            crossing = jnp.where(upper, low, high)
            crossed = jnp.take_along_axis(crossing, lane ^ step, axis=1, mode="promise_in_bounds")
            rows[i] = jnp.where(upper, crossed, low)
            rows[i | (1 << bit)] = jnp.where(upper, high, crossed)
    return rows


def pack_group(rows_of, out_ref, group):
    rows = [rows_of(b) for b in range(RANKS)]
    for rank, row in enumerate(swap_blocks(rows)):
        out_ref[rank, group] = row


def pack_kernel(
    fields_hbm,
    forcing_hbm,
    weights_hbm,
    east_hbm,
    north_hbm,
    damping_hbm,
    depths_hbm,
    links_ref,
    out_hbm,
    fields_ref,
    forcing_ref,
    weights_ref,
    east_ref,
    north_ref,
    damping_ref,
    depths_ref,
    rows_ref,
    out_ref,
    sems,
    out_sems,
):
    sources = (fields_hbm, forcing_hbm, weights_hbm, east_hbm, north_hbm, damping_hbm, depths_hbm)
    targets = (fields_ref, forcing_ref, weights_ref, east_ref, north_ref, damping_ref, depths_ref)
    copies = [pltpu.make_async_copy(a, b, sems.at[i]) for i, (a, b) in enumerate(zip(sources, targets))]
    for copy in copies:
        copy.start()
    first = lax.axis_index("node") * RANKS
    for link in range(2):
        for b in range(RANKS):
            local = (links_ref[2 + link, b] - first).astype(jnp.float32)
            at = ROW_LINKS + link
            rows_ref[at, :, LANES * b : LANES * (b + 1)] = jnp.full((1, LANES), local, jnp.float32)
    sent = []

    def send(index, group, count):
        part = pl.ds(group, count)
        copy = pltpu.make_async_copy(out_ref.at[:, part], out_hbm.at[:, part], out_sems.at[index])
        copy.start()
        sent.append(copy)

    for group in range(6):
        if group % 3 == 0:
            copies[group // 3].wait()
        source = (fields_ref, forcing_ref)[group // 3]

        def block(b):
            start = 32 * (group % 3) + 2 * b
            parts = [source[pl.ds(start + part, 4, stride=96), :] for part in range(2)]
            return jnp.concatenate(parts, axis=0)

        pack_group(block, out_ref, group)
        if group % 3 == 2:
            send(group // 3, group - 2, 3)
    for copy in copies[2:]:
        copy.wait()
    for kind, source in enumerate((weights_ref, east_ref, north_ref)):
        for link in range(4):
            rows_ref[4 * kind + link] = source[link : link + 1, :]
    rows_ref[ROW_DAMPING] = damping_ref[...]
    rows_ref[ROW_DEPTHS] = depths_ref[...]
    mine = lax.axis_index("freq")
    rows = [jnp.broadcast_to(rows_ref[mine, :, LANES * b : LANES * (b + 1)], (8, LANES)) for b in range(RANKS)]
    diagonal = jnp.sum(weights_ref[...], axis=0, keepdims=True) + (2.0 / 3.0) * damping_ref[...] + ETA_DAMP / 3.0
    mean = jnp.sum(diagonal, axis=1, keepdims=True) * (1.0 / diagonal.shape[1])
    top = iota((8, LANES), 0) == 0
    for rank, row in enumerate(swap_blocks(rows)):
        out_ref[rank, 6] = jnp.where(top, row, mean)
    send(2, 6, 1)
    for copy in sent:
        copy.wait()


def forward_kernel(given_ref, _, out_ref):
    for half in range(2):
        rows = jnp.concatenate([given_ref[8 * half + i, 6, 0:1] for i in range(8)], axis=0)
        for rank in range(RANKS):
            out_ref[rank, 3 + half] = rows
    for rank in range(RANKS):
        for comp in range(3):
            out_ref[rank, comp] = given_ref[rank, comp]


def unpack_kernel(x_ref, fields_hbm, residual_hbm, fields_ref, residual_ref, sems):
    copies = []
    for i, (target, out) in enumerate(((fields_ref, fields_hbm), (residual_ref, residual_hbm))):
        for comp in range(3):
            rows = swap_blocks([x_ref[rank, 3 * i + comp] for rank in range(RANKS)])
            for b, row in enumerate(rows):
                for part in range(2):
                    target[pl.ds(32 * comp + 2 * b + part, 4, stride=96), :] = row[4 * part : 4 * part + 4]
        copies.append(pltpu.make_async_copy(target, out, sems.at[i]))
        copies[-1].start()
    for copy in copies:
        copy.wait()


def tables_kernel(harmonic_ref, cosines_ref, synthesis_ref, analysis_ref):
    samples = iota((SAMPLES, LANES), 0)
    quarter = jnp.where((iota((SAMPLES, LANES), 1) & 4) != 0, SAMPLES // 4, 0)
    harmonic = jnp.broadcast_to(harmonic_ref[...], (SAMPLES, LANES))
    turn = (samples * harmonic + quarter) & (SAMPLES - 1)
    cosines = jnp.broadcast_to(cosines_ref[...], (SAMPLES, LANES))
    synthesis = jnp.take_along_axis(cosines, turn, axis=1, mode="promise_in_bounds")
    synthesis_ref[...] = synthesis
    analysis_ref[...] = (synthesis * jnp.where(harmonic == 0, 1.0 / SAMPLES, 2.0 / SAMPLES)).T


def friction_kernel(x_ref, table_ref, synthesis_ref, analysis_ref, out_ref):
    moments = [
        jnp.dot(
            synthesis_ref[...],
            x_ref[:, comp].reshape(LANES, LANES),
            precision=TOP_HARMONIC,
            preferred_element_type=jnp.float32,
        )
        for comp in range(3)
    ]
    elevation, eastward, northward = moments
    group = lax.axis_index("freq")
    depths = table_ref[ROW_DEPTHS, 3 + group // 8]
    depth = jnp.sum(jnp.where(iota((8, LANES), 0) == group % 8, depths, 0.0), axis=0, keepdims=True)
    column_depth = depth + 0.5 * jnp.tanh(elevation)
    magnitude = jnp.sqrt(eastward * eastward + northward * northward + SPEED_FLOOR)
    factor = FRICTION * magnitude / column_depth
    for comp, moving in enumerate((eastward, northward)):
        terms = jnp.dot(
            analysis_ref[...], factor * moving, precision=TOP_HARMONIC, preferred_element_type=jnp.float32
        )
        out_ref[:, comp] = terms.reshape(RANKS, 8, LANES)


def prepare_links(table_ref, shift, links_ref, index_ref):
    share = iota((8, LANES), 1) & (SHARE - 1)
    for half in range(2):
        rows = [table_ref[at, 3 + half] for at in range(RANKS)]
        spread = rows[0] + rows[1] + rows[2] + rows[3]
        values = rows[:12] + [
            spread + (ETA_DAMP - shift),
            spread + (rows[ROW_DAMPING] - shift),
            rows[4] + rows[5] + rows[6] + rows[7],
            rows[8] + rows[9] + rows[10] + rows[11],
        ]
        for i in range(8):
            for at, value in enumerate(values):
                links_ref[8 * half + i, at] = jnp.broadcast_to(value[i : i + 1], (8, LANES))
        for link in range(2):
            at = rows[ROW_LINKS + link].astype(jnp.int32)
            outside = jnp.logical_or(at < 0, at > RANKS - 1)
            lane = (at & (RANKS - 1)) * SHARE + share
            index = jnp.where(outside, lane + LANES, lane)
            for i in range(8):
                index_ref[8 * half + i, link] = jnp.broadcast_to(index[i : i + 1], (8, LANES))


def apply_operator(vectors, links_ref, index_ref):
    lane = iota((8, LANES), 1)
    first = lane < SHARE
    last = lane >= LANES - SHARE
    result = []
    for g in range(RANKS):
        here = vectors[g]
        before = vectors[g - 1] if g > 0 else [pltpu.roll(x, LANES - 2 * SHARE, 1) for x in here]
        after = vectors[g + 1] if g < RANKS - 1 else [pltpu.roll(x, 2 * SHARE, 1) for x in here]
        beside = []
        beside.append([pltpu.roll(jnp.where(last, p, x), SHARE, 1) for p, x in zip(before, here)])
        beside.append([pltpu.roll(jnp.where(first, n, x), LANES - SHARE, 1) for n, x in zip(after, here)])
        edges = [jnp.where(last, p, n) for p, n in zip(before, after)]
        for link in range(2):
            index = index_ref[g, link]
            outside = index >= LANES
            index = index & (LANES - 1)
            beside.append(
                [
                    jnp.where(
                        outside,
                        jnp.take_along_axis(e, index, axis=1, mode="promise_in_bounds"),
                        jnp.take_along_axis(x, index, axis=1, mode="promise_in_bounds"),
                    )
                    for e, x in zip(edges, here)
                ]
            )
        x_ele, x_east, x_north = here
        eta_sum, flow_sum, east_sum, north_sum = [links_ref[g, 12 + at] for at in range(4)]
        ele = eta_sum * x_ele - east_sum * x_east - north_sum * x_north
        east = flow_sum * x_east - east_sum * x_ele - CORIOLIS * x_north
        north = flow_sum * x_north - north_sum * x_ele + CORIOLIS * x_east
        for link in range(4):
            y_ele, y_east, y_north = beside[link]
            weight, to_east, to_north = [links_ref[g, at + link] for at in (0, 4, 8)]
            ele = ele - weight * y_ele + to_east * y_east + to_north * y_north
            east = east - weight * y_east + to_east * y_ele
            north = north - weight * y_north + to_north * y_ele
        result.append([ele, east, north])
    return result


def slot_rows(ref, pick):
    first = lax.axis_index("freq") * 4
    slot = iota((8, LANES), 0) & 3
    values = [pick(ref, first + s) for s in range(4)]
    return jnp.where(slot == 0, values[0], jnp.where(slot == 1, values[1], jnp.where(slot == 2, values[2], values[3])))


def angular_rows(harmonic_ref):
    return OMEGA_STEP * slot_rows(harmonic_ref, lambda ref, i: ref[i]).astype(jnp.float32)


def start_kernel(given_ref, table_ref, harmonic_ref, base_ref, links_ref, index_ref, shift_ref):
    shift = given_ref[0, 6, 1:2]
    for g in range(1, RANKS):
        shift = shift + given_ref[g, 6, 1:2]
    shift = jnp.broadcast_to(shift * (1.0 / RANKS), (8, LANES))
    shift_ref[...] = shift
    prepare_links(table_ref, shift, links_ref, index_ref)
    turn = angular_rows(harmonic_ref) * jnp.where(iota((8, LANES), 0) < 4, -1.0, 1.0)
    vectors = [[given_ref[g, comp] for comp in range(3)] for g in range(RANKS)]
    images = apply_operator(vectors, links_ref, index_ref)
    for g in range(RANKS):
        for comp in range(3):
            rest = shift * vectors[g][comp] + turn * pltpu.roll(vectors[g][comp], 4, 0)
            base_ref[g, comp] = given_ref[g, 3 + comp] - images[g][comp] - rest


def basis_kernel(base_ref, friction_ref, links_ref, index_ref, basis_ref, gram_ref, swap_ref):
    for g in range(RANKS):
        basis_ref[0, g, 0] = base_ref[g, 0]
        basis_ref[0, g, 1] = base_ref[g, 1] - friction_ref[g, 0]
        basis_ref[0, g, 2] = base_ref[g, 2] - friction_ref[g, 1]

    def power(m, _):
        vectors = [[basis_ref[m, g, comp] for comp in range(3)] for g in range(RANKS)]
        images = apply_operator(vectors, links_ref, index_ref)
        for g in range(RANKS):
            for comp in range(3):
                basis_ref[m + 1, g, comp] = images[g][comp]
                swap_ref[m, g, comp, pl.ds(0, 8, stride=2), :] = images[g][comp]
                swap_ref[m, g, comp, pl.ds(16, 8, stride=2), :] = images[g][comp]
        return 0

    lax.fori_loop(0, LMAX, power, 0)

    def products(g, sums):
        for comp in range(3):
            vectors = [basis_ref[m, g, comp] for m in range(COUNT)]
            turned = [None] + [swap_ref[m, g, comp, pl.ds(8, 8, stride=2), :] for m in range(LMAX)]
            terms = [vectors[m] * vectors[n] for m, n in REAL_PAIRS]
            terms += [vectors[m] * turned[n] for m, n in IMAG_PAIRS]
            sums = tuple(a + b for a, b in zip(sums, terms))
        return sums

    entries = len(REAL_PAIRS) + len(IMAG_PAIRS)
    sums = lax.fori_loop(0, RANKS, products, tuple(jnp.zeros((8, LANES), jnp.float32) for _ in range(entries)))
    lane = iota((8, LANES), 1)
    gram = jnp.zeros((8, LANES), jnp.float32)
    for entry, value in enumerate(sums):
        gram = jnp.where(lane == entry, jnp.sum(value, axis=1, keepdims=True), gram)
    turned = pltpu.roll(gram, 4, 0)
    gram = jnp.where(lane < len(REAL_PAIRS), gram + turned, gram - turned)
    packed = jnp.where(lane < LANES // 2, gram, pltpu.roll(pltpu.roll(gram, LANES // 2, 1), 6, 0))[:2]
    for rank in range(RANKS):
        gram_ref[rank] = packed


def step_sizes(gram_ref, shift, harmonic_ref, counts_ref, sweep):
    gram = gram_ref[0]
    for rank in range(1, RANKS):
        gram = gram + gram_ref[rank]
    swapped = pltpu.roll(gram, LANES // 2, 1)
    gram = jnp.concatenate([gram, swapped, gram, swapped], axis=0)

    def entry(values, at):
        return jnp.broadcast_to(values[:, at : at + 1], (8, LANES))

    inner = {}
    for at, (m, n) in enumerate(REAL_PAIRS):
        inner[m, n] = (entry(gram, at), None)
    for at, (m, n) in enumerate(IMAG_PAIRS):
        inner[m, n] = (inner[m, n][0], entry(gram, len(REAL_PAIRS) + at))

    def mul(a, b):
        return (a[0] * b[0] - a[1] * b[1], a[0] * b[1] + a[1] * b[0])

    def add(a, b):
        return (a[0] + b[0], a[1] + b[1])

    def conj_mul(a, b):
        return (a[0] * b[0] + a[1] * b[1], a[0] * b[1] - a[1] * b[0])

    def gram_times(m, n, b):
        if m == n:
            g = inner[m, n][0]
            return (g * b[0], g * b[1])
        if m < n:
            return mul(inner[m, n], b)
        return conj_mul(inner[n, m], b)

    angular = angular_rows(harmonic_ref)
    counts = slot_rows(counts_ref, lambda ref, i: ref[sweep, i])
    zero = jnp.zeros((8, LANES), jnp.float32)
    residual = [(jnp.ones((8, LANES), jnp.float32), zero)]
    correction = [(zero, zero) for _ in range(LMAX)]
    for step in range(LMAX):
        image = []
        for m in range(step + 2):
            value = (zero, zero)
            if m <= step:
                r = residual[m]
                value = (shift * r[0] - angular * r[1], shift * r[1] + angular * r[0])
            if m > 0:
                value = add(value, residual[m - 1])
            image.append(value)
        upper = (zero, zero)
        lower = zero
        for m in range(step + 2):
            with_residual = (zero, zero)
            for n in range(step + 1):
                with_residual = add(with_residual, gram_times(m, n, residual[n]))
            upper = add(upper, conj_mul(image[m], with_residual))
            with_image = (zero, zero)
            for n in range(step + 2):
                with_image = add(with_image, gram_times(m, n, image[n]))
            lower = lower + image[m][0] * with_image[0] + image[m][1] * with_image[1]
        lower = lower + 1e-06
        active = jnp.where(step < counts, 1.0, 0.0)
        alpha = (active * upper[0] / lower, active * upper[1] / lower)
        for m in range(step + 1):
            correction[m] = add(correction[m], mul(alpha, residual[m]))
        residual = residual + [(zero, zero)]
        for m in range(step + 2):
            change = mul(alpha, image[m])
            residual[m] = (residual[m][0] - change[0], residual[m][1] - change[1])
    return correction, residual


def combine(coefs, vectors, sign):
    straight = coefs[0][0] * vectors[0]
    turned = coefs[0][1] * vectors[0]
    for (real, imag), vector in zip(coefs[1:], vectors[1:]):
        straight = straight + real * vector
        turned = turned + imag * vector
    return straight + sign * pltpu.roll(turned, 4, 0)


def update_kernel(sweep, gram_ref, fields_ref, basis_ref, friction_ref, shift_ref, harmonic_ref, counts_ref, *outs):
    correction, residual = step_sizes(gram_ref, shift_ref[...], harmonic_ref, counts_ref, sweep)
    sign = jnp.where(iota((8, LANES), 0) < 4, -1.0, 1.0)

    def update(g, _):
        for comp in range(3):
            vectors = [basis_ref[m, g, comp] for m in range(COUNT)]
            fields = fields_ref[g, comp] + combine(correction, vectors[:LMAX], sign)
            left = combine(residual, vectors, sign)
            if sweep == SWEEPS - 1:
                outs[0][g, comp] = fields
                outs[0][g, 3 + comp] = left
            else:
                outs[0][g, comp] = fields
                outs[1][g, comp] = left if comp == 0 else left + friction_ref[g, comp - 1]
        return 0

    lax.fori_loop(0, RANKS, update, 0)


def struct(*shape):
    return jax.ShapeDtypeStruct(shape, jnp.float32)


def call(kernel, out, specs, scratch=(), mebibytes=16, out_specs=None):
    outs = out if isinstance(out, list) else [out]
    result = pl.pallas_call(
        kernel,
        out_shape=outs,
        in_specs=specs,
        out_specs=out_specs or [VMEM] * len(outs),
        scratch_shapes=list(scratch),
        compiler_params=pltpu.CompilerParams(vmem_limit_bytes=mebibytes * 1024 * 1024),
    )
    return (lambda *args: result(*args)) if isinstance(out, list) else (lambda *args: result(*args)[0])


def exchange(values, axis):
    return lax.all_to_all(values, axis, split_axis=0, concat_axis=0, tiled=True)


def rows_of(x):
    return x.transpose(0, 2, 1, 3).reshape(4, 3, 2, RANKS, LANES).transpose(0, 1, 3, 2, 4).reshape(-1, LANES)


def fields_of(rows):
    return rows.reshape(4, 3, RANKS, 2, LANES).transpose(0, 3, 1, 2, 4).reshape(4, 2, 3, RANKS * LANES)


def body(
    harmonics, forcing, depths, damping, weights, couple_east, couple_north, connections, counts, harmonic_of_slot
):
    whole = pltpu.VMEM((384, LANES), jnp.float32)
    four = pltpu.VMEM((4, 2048), jnp.float32)
    line = pltpu.VMEM((1, 2048), jnp.float32)
    packed = call(
        pack_kernel,
        struct(RANKS, 7, 8, LANES),
        [HBM] * 7 + [SMEM],
        (
            whole,
            whole,
            four,
            four,
            four,
            line,
            line,
            pltpu.VMEM((RANKS, 1, 2048), jnp.float32),
            pltpu.VMEM((RANKS, 7, 8, LANES), jnp.float32),
            pltpu.SemaphoreType.DMA((7,)),
            pltpu.SemaphoreType.DMA((3,)),
        ),
        58,
        [HBM],
    )(
        rows_of(harmonics),
        rows_of(forcing),
        weights,
        couple_east,
        couple_north,
        damping.reshape(1, -1),
        depths.reshape(1, -1),
        connections.T,
    )
    given = exchange(packed, "node")
    slots = jnp.broadcast_to(harmonic_of_slot.reshape(RANKS, 1, 4), (RANKS, 2, 4)).reshape(1, LANES)
    cosines = np.cos(np.arange(SAMPLES) * (2.0 * math.pi / SAMPLES)).astype(np.float32).reshape(1, SAMPLES)

    synthesis, analysis = call(tables_kernel, [struct(SAMPLES, LANES), struct(LANES, SAMPLES)], [VMEM] * 2)(
        slots, cosines
    )
    table = exchange(call(forward_kernel, struct(RANKS, 5, 8, LANES), [VMEM, HBM])(given, analysis), "freq")

    def friction_of(received):
        terms = call(friction_kernel, struct(RANKS, 2, 8, LANES), [VMEM] * 4)(received, table, synthesis, analysis)
        return exchange(terms, "freq")

    base, links, index, shift = call(
        start_kernel,
        [
            struct(RANKS, 3, 8, LANES),
            struct(RANKS, 16, 8, LANES),
            jax.ShapeDtypeStruct((RANKS, 2, 8, LANES), jnp.int32),
            struct(8, LANES),
        ],
        [VMEM, VMEM, SMEM],
    )(given, table, harmonic_of_slot)
    fields = given
    friction = friction_of(table)
    for sweep in range(SWEEPS):
        basis, gram = call(
            basis_kernel,
            [struct(COUNT, RANKS, 3, 8, LANES), struct(RANKS, 2, LANES)],
            [VMEM] * 4,
            (pltpu.VMEM((LMAX, RANKS, 3, 32, LANES), jnp.float32),),
        )(base, friction, links, index)
        gram = exchange(gram, "node")
        if sweep < SWEEPS - 1:
            outs = [struct(RANKS, 3, 8, LANES), struct(RANKS, 3, 8, LANES)]
        else:
            outs = [struct(RANKS, 6, 8, LANES)]
        results = call(functools.partial(update_kernel, sweep), outs, [VMEM] * 5 + [SMEM] * 2)(
            gram, fields, basis, friction, shift, harmonic_of_slot, counts
        )
        if sweep < SWEEPS - 1:
            fields, base = results
            friction = friction_of(exchange(fields, "freq"))
    out = [struct(384, LANES)] * 2
    fields, residual = call(
        unpack_kernel, out, [VMEM], (whole, whole, pltpu.SemaphoreType.DMA((2,))), 16, [HBM] * 2
    )(exchange(results[0], "node"))
    return (fields_of(fields), fields_of(residual))


def solution(mesh):
    return jax.shard_map(
        body,
        mesh=mesh,
        in_specs=(
            P("freq", None, None, "node"),
            P("freq", None, None, "node"),
            P("node"),
            P("node"),
            P(None, "node"),
            P(None, "node"),
            P(None, "node"),
            P("node", None),
            P(),
            P(),
        ),
        out_specs=(P("freq", None, None, "node"), P("freq", None, None, "node")),
        check_vma=False,
    )
```

```python
import functools
import math

import jax
import jax.numpy as jnp
import numpy as np
from jax import lax
from jax.experimental import pallas as pl
from jax.experimental.pallas import tpu as pltpu
from jax.sharding import PartitionSpec as P

SAMPLES = 128
LMAX = 5
SWEEPS = 2

FRICTION = 2.0
CORIOLIS = 0.5
ETA_DAMP = 0.2
OMEGA_STEP = 0.05
SPEED_FLOOR = 0.01
TOP_HARMONIC = lax.Precision.HIGHEST

RANKS = 16
LANES = 128
SHARE = 8
COUNT = LMAX + 1
REAL_PAIRS = [(m, n) for m in range(COUNT) for n in range(m, COUNT)]
IMAG_PAIRS = [(m, n) for m in range(COUNT) for n in range(m + 1, COUNT)]
ROW_DAMPING, ROW_DEPTHS, ROW_LINKS = 12, 13, 14

VMEM = pl.BlockSpec(memory_space=pltpu.VMEM)
HBM = pl.BlockSpec(memory_space=pl.ANY)
SMEM = pl.BlockSpec(memory_space=pltpu.SMEM)


def iota(shape, axis):
    return lax.broadcasted_iota(jnp.int32, shape, axis)


def swap_blocks(rows):
    lane = iota((8, LANES), 1)
    rows = list(rows)
    for bit in range(4):
        step = SHARE << bit
        upper = (lane & step) != 0
        for i in range(RANKS):
            if i & (1 << bit):
                continue
            low, high = rows[i], rows[i | (1 << bit)]
            crossing = jnp.where(upper, low, high)
            crossed = jnp.take_along_axis(crossing, lane ^ step, axis=1, mode="promise_in_bounds")
            rows[i] = jnp.where(upper, crossed, low)
            rows[i | (1 << bit)] = jnp.where(upper, high, crossed)
    return rows


def pack_group(rows_of, out_ref, group):
    rows = [rows_of(b) for b in range(RANKS)]
    for rank, row in enumerate(swap_blocks(rows)):
        out_ref[rank, group] = row


def pack_kernel(
    fields_hbm,
    forcing_hbm,
    weights_hbm,
    east_hbm,
    north_hbm,
    damping_hbm,
    depths_hbm,
    links_hbm,
    out_hbm,
    fields_ref,
    forcing_ref,
    weights_ref,
    east_ref,
    north_ref,
    damping_ref,
    depths_ref,
    links_ref,
    rows_ref,
    out_ref,
    sems,
    out_sems,
):
    sources = (fields_hbm, forcing_hbm, weights_hbm, east_hbm, north_hbm, damping_hbm, depths_hbm, links_hbm)
    targets = (fields_ref, forcing_ref, weights_ref, east_ref, north_ref, damping_ref, depths_ref, links_ref)
    copies = [pltpu.make_async_copy(a, b, sems.at[i]) for i, (a, b) in enumerate(zip(sources, targets))]
    for copy in copies:
        copy.start()
    sent = []

    def send(index, group, count):
        part = pl.ds(group, count)
        copy = pltpu.make_async_copy(out_ref.at[:, part], out_hbm.at[:, part], out_sems.at[index])
        copy.start()
        sent.append(copy)

    for group in range(6):
        if group % 3 == 0:
            copies[group // 3].wait()
        source = (fields_ref, forcing_ref)[group // 3]

        def block(b):
            start = 32 * (group % 3) + 2 * b
            parts = [source[pl.ds(start + part, 4, stride=96), :] for part in range(2)]
            return jnp.concatenate(parts, axis=0)

        pack_group(block, out_ref, group)
        if group % 3 == 2:
            send(group // 3, group - 2, 3)
    for copy in copies[2:]:
        copy.wait()
    for kind, source in enumerate((weights_ref, east_ref, north_ref)):
        for link in range(4):
            rows_ref[4 * kind + link] = source[link : link + 1, :]
    rows_ref[ROW_DAMPING] = damping_ref[...]
    rows_ref[ROW_DEPTHS] = depths_ref[...]
    local = (links_ref[...] - lax.axis_index("node") * RANKS).astype(jnp.float32)
    for link in range(2):
        for b in range(RANKS):
            row = jnp.broadcast_to(local[2 + link : 3 + link, b : b + 1], (1, LANES))
            rows_ref[ROW_LINKS + link, :, LANES * b : LANES * (b + 1)] = row
    mine = lax.axis_index("freq")
    rows = [jnp.broadcast_to(rows_ref[mine, :, LANES * b : LANES * (b + 1)], (8, LANES)) for b in range(RANKS)]
    diagonal = jnp.sum(weights_ref[...], axis=0, keepdims=True) + (2.0 / 3.0) * damping_ref[...] + ETA_DAMP / 3.0
    mean = jnp.sum(diagonal, axis=1, keepdims=True) * (1.0 / diagonal.shape[1])
    top = iota((8, LANES), 0) == 0
    for rank, row in enumerate(swap_blocks(rows)):
        out_ref[rank, 6] = jnp.where(top, row, mean)
    send(2, 6, 1)
    for copy in sent:
        copy.wait()


def forward_kernel(given_ref, _, out_ref):
    for half in range(2):
        rows = jnp.concatenate([given_ref[8 * half + i, 6, 0:1] for i in range(8)], axis=0)
        for rank in range(RANKS):
            out_ref[rank, 3 + half] = rows
    for rank in range(RANKS):
        for comp in range(3):
            out_ref[rank, comp] = given_ref[rank, comp]


def unpack_kernel(x_ref, fields_hbm, residual_hbm, fields_ref, residual_ref, sems):
    copies = []
    for i, (target, out) in enumerate(((fields_ref, fields_hbm), (residual_ref, residual_hbm))):
        for comp in range(3):
            rows = swap_blocks([x_ref[rank, 3 * i + comp] for rank in range(RANKS)])
            for b, row in enumerate(rows):
                for part in range(2):
                    target[pl.ds(32 * comp + 2 * b + part, 4, stride=96), :] = row[4 * part : 4 * part + 4]
        copies.append(pltpu.make_async_copy(target, out, sems.at[i]))
        copies[-1].start()
    for copy in copies:
        copy.wait()


def tables_kernel(harmonic_ref, cosines_ref, synthesis_ref, analysis_ref):
    samples = iota((SAMPLES, LANES), 0)
    quarter = jnp.where((iota((SAMPLES, LANES), 1) & 4) != 0, SAMPLES // 4, 0)
    harmonic = jnp.broadcast_to(harmonic_ref[...], (SAMPLES, LANES))
    turn = (samples * harmonic + quarter) & (SAMPLES - 1)
    cosines = jnp.broadcast_to(cosines_ref[...], (SAMPLES, LANES))
    synthesis = jnp.take_along_axis(cosines, turn, axis=1, mode="promise_in_bounds")
    synthesis_ref[...] = synthesis
    analysis_ref[...] = (synthesis * jnp.where(harmonic == 0, 1.0 / SAMPLES, 2.0 / SAMPLES)).T


def friction_kernel(x_ref, table_ref, synthesis_ref, analysis_ref, out_ref):
    moments = [
        jnp.dot(
            synthesis_ref[...],
            x_ref[:, comp].reshape(LANES, LANES),
            precision=TOP_HARMONIC,
            preferred_element_type=jnp.float32,
        )
        for comp in range(3)
    ]
    elevation, eastward, northward = moments
    group = lax.axis_index("freq")
    depths = table_ref[ROW_DEPTHS, 3 + group // 8]
    depth = jnp.sum(jnp.where(iota((8, LANES), 0) == group % 8, depths, 0.0), axis=0, keepdims=True)
    column_depth = depth + 0.5 * jnp.tanh(elevation)
    magnitude = jnp.sqrt(eastward * eastward + northward * northward + SPEED_FLOOR)
    factor = FRICTION * magnitude / column_depth
    for comp, moving in enumerate((eastward, northward)):
        terms = jnp.dot(
            analysis_ref[...], factor * moving, precision=TOP_HARMONIC, preferred_element_type=jnp.float32
        )
        out_ref[:, comp] = terms.reshape(RANKS, 8, LANES)


def prepare_links(table_ref, shift, links_ref, index_ref):
    share = iota((8, LANES), 1) & (SHARE - 1)
    for half in range(2):
        rows = [table_ref[at, 3 + half] for at in range(RANKS)]
        spread = rows[0] + rows[1] + rows[2] + rows[3]
        values = rows[:12] + [
            spread + (ETA_DAMP - shift),
            spread + (rows[ROW_DAMPING] - shift),
            rows[4] + rows[5] + rows[6] + rows[7],
            rows[8] + rows[9] + rows[10] + rows[11],
        ]
        for i in range(8):
            for at, value in enumerate(values):
                links_ref[8 * half + i, at] = jnp.broadcast_to(value[i : i + 1], (8, LANES))
        for link in range(2):
            at = rows[ROW_LINKS + link].astype(jnp.int32)
            outside = jnp.logical_or(at < 0, at > RANKS - 1)
            lane = (at & (RANKS - 1)) * SHARE + share
            index = jnp.where(outside, lane + LANES, lane)
            for i in range(8):
                index_ref[8 * half + i, link] = jnp.broadcast_to(index[i : i + 1], (8, LANES))


def apply_operator(vectors, links_ref, index_ref):
    lane = iota((8, LANES), 1)
    first = lane < SHARE
    last = lane >= LANES - SHARE
    result = []
    for g in range(RANKS):
        here = vectors[g]
        before = vectors[g - 1] if g > 0 else [pltpu.roll(x, LANES - 2 * SHARE, 1) for x in here]
        after = vectors[g + 1] if g < RANKS - 1 else [pltpu.roll(x, 2 * SHARE, 1) for x in here]
        beside = []
        beside.append([pltpu.roll(jnp.where(last, p, x), SHARE, 1) for p, x in zip(before, here)])
        beside.append([pltpu.roll(jnp.where(first, n, x), LANES - SHARE, 1) for n, x in zip(after, here)])
        edges = [jnp.where(last, p, n) for p, n in zip(before, after)]
        for link in range(2):
            index = index_ref[g, link]
            outside = index >= LANES
            index = index & (LANES - 1)
            beside.append(
                [
                    jnp.where(
                        outside,
                        jnp.take_along_axis(e, index, axis=1, mode="promise_in_bounds"),
                        jnp.take_along_axis(x, index, axis=1, mode="promise_in_bounds"),
                    )
                    for e, x in zip(edges, here)
                ]
            )
        x_ele, x_east, x_north = here
        eta_sum, flow_sum, east_sum, north_sum = [links_ref[g, 12 + at] for at in range(4)]
        ele = eta_sum * x_ele - east_sum * x_east - north_sum * x_north
        east = flow_sum * x_east - east_sum * x_ele - CORIOLIS * x_north
        north = flow_sum * x_north - north_sum * x_ele + CORIOLIS * x_east
        for link in range(4):
            y_ele, y_east, y_north = beside[link]
            weight, to_east, to_north = [links_ref[g, at + link] for at in (0, 4, 8)]
            ele = ele - weight * y_ele + to_east * y_east + to_north * y_north
            east = east - weight * y_east + to_east * y_ele
            north = north - weight * y_north + to_north * y_ele
        result.append([ele, east, north])
    return result


def slot_rows(ref, pick):
    first = lax.axis_index("freq") * 4
    slot = iota((8, LANES), 0) & 3
    values = [pick(ref, first + s) for s in range(4)]
    return jnp.where(slot == 0, values[0], jnp.where(slot == 1, values[1], jnp.where(slot == 2, values[2], values[3])))


def angular_rows(harmonic_ref):
    return OMEGA_STEP * slot_rows(harmonic_ref, lambda ref, i: ref[i]).astype(jnp.float32)


def start_kernel(given_ref, table_ref, harmonic_ref, counts_ref, base_ref, links_ref, index_ref, slots_ref):
    shift = given_ref[0, 6, 1:2]
    for g in range(1, RANKS):
        shift = shift + given_ref[g, 6, 1:2]
    shift = jnp.broadcast_to(shift * (1.0 / RANKS), (8, LANES))
    angular = angular_rows(harmonic_ref)
    slots_ref[0] = shift
    slots_ref[1] = angular
    for sweep in range(SWEEPS):
        slots_ref[2 + sweep] = slot_rows(counts_ref, lambda ref, i: ref[sweep, i]).astype(jnp.float32)
    prepare_links(table_ref, shift, links_ref, index_ref)
    turn = angular * jnp.where(iota((8, LANES), 0) < 4, -1.0, 1.0)
    vectors = [[given_ref[g, comp] for comp in range(3)] for g in range(RANKS)]
    images = apply_operator(vectors, links_ref, index_ref)
    for g in range(RANKS):
        for comp in range(3):
            rest = shift * vectors[g][comp] + turn * pltpu.roll(vectors[g][comp], 4, 0)
            base_ref[g, comp] = given_ref[g, 3 + comp] - images[g][comp] - rest


def basis_kernel(base_ref, friction_ref, links_ref, index_ref, basis_ref, gram_ref, swap_ref):
    for g in range(RANKS):
        basis_ref[0, g, 0] = base_ref[g, 0]
        basis_ref[0, g, 1] = base_ref[g, 1] - friction_ref[g, 0]
        basis_ref[0, g, 2] = base_ref[g, 2] - friction_ref[g, 1]

    def power(m, _):
        vectors = [[basis_ref[m, g, comp] for comp in range(3)] for g in range(RANKS)]
        images = apply_operator(vectors, links_ref, index_ref)
        for g in range(RANKS):
            for comp in range(3):
                basis_ref[m + 1, g, comp] = images[g][comp]
                swap_ref[m, g, comp, pl.ds(0, 8, stride=2), :] = images[g][comp]
                swap_ref[m, g, comp, pl.ds(16, 8, stride=2), :] = images[g][comp]
        return 0

    lax.fori_loop(0, LMAX, power, 0)

    def products(g, sums):
        for comp in range(3):
            vectors = [basis_ref[m, g, comp] for m in range(COUNT)]
            turned = [None] + [swap_ref[m, g, comp, pl.ds(8, 8, stride=2), :] for m in range(LMAX)]
            terms = [vectors[m] * vectors[n] for m, n in REAL_PAIRS]
            terms += [vectors[m] * turned[n] for m, n in IMAG_PAIRS]
            sums = tuple(a + b for a, b in zip(sums, terms))
        return sums

    entries = len(REAL_PAIRS) + len(IMAG_PAIRS)
    sums = lax.fori_loop(0, RANKS, products, tuple(jnp.zeros((8, LANES), jnp.float32) for _ in range(entries)))
    lane = iota((8, LANES), 1)
    gram = jnp.zeros((8, LANES), jnp.float32)
    for entry, value in enumerate(sums):
        gram = jnp.where(lane == entry, jnp.sum(value, axis=1, keepdims=True), gram)
    turned = pltpu.roll(gram, 4, 0)
    gram = jnp.where(lane < len(REAL_PAIRS), gram + turned, gram - turned)
    packed = jnp.where(lane < LANES // 2, gram, pltpu.roll(pltpu.roll(gram, LANES // 2, 1), 6, 0))[:2]
    for rank in range(RANKS):
        gram_ref[rank] = packed


def step_sizes(gram_ref, slots_ref, sweep):
    gram = gram_ref[0]
    for rank in range(1, RANKS):
        gram = gram + gram_ref[rank]
    swapped = pltpu.roll(gram, LANES // 2, 1)
    gram = jnp.concatenate([gram, swapped, gram, swapped], axis=0)

    def entry(values, at):
        return jnp.broadcast_to(values[:, at : at + 1], (8, LANES))

    inner = {}
    for at, (m, n) in enumerate(REAL_PAIRS):
        inner[m, n] = (entry(gram, at), None)
    for at, (m, n) in enumerate(IMAG_PAIRS):
        inner[m, n] = (inner[m, n][0], entry(gram, len(REAL_PAIRS) + at))

    def mul(a, b):
        return (a[0] * b[0] - a[1] * b[1], a[0] * b[1] + a[1] * b[0])

    def add(a, b):
        return (a[0] + b[0], a[1] + b[1])

    def conj_mul(a, b):
        return (a[0] * b[0] + a[1] * b[1], a[0] * b[1] - a[1] * b[0])

    def gram_times(m, n, b):
        if m == n:
            g = inner[m, n][0]
            return (g * b[0], g * b[1])
        if m < n:
            return mul(inner[m, n], b)
        return conj_mul(inner[n, m], b)

    shift, angular, counts = slots_ref[0], slots_ref[1], slots_ref[2 + sweep]
    zero = jnp.zeros((8, LANES), jnp.float32)
    residual = [(jnp.ones((8, LANES), jnp.float32), zero)]
    correction = [(zero, zero) for _ in range(LMAX)]
    for step in range(LMAX):
        image = []
        for m in range(step + 2):
            value = (zero, zero)
            if m <= step:
                r = residual[m]
                value = (shift * r[0] - angular * r[1], shift * r[1] + angular * r[0])
            if m > 0:
                value = add(value, residual[m - 1])
            image.append(value)
        upper = (zero, zero)
        lower = zero
        for m in range(step + 2):
            with_residual = (zero, zero)
            for n in range(step + 1):
                with_residual = add(with_residual, gram_times(m, n, residual[n]))
            upper = add(upper, conj_mul(image[m], with_residual))
            with_image = (zero, zero)
            for n in range(step + 2):
                with_image = add(with_image, gram_times(m, n, image[n]))
            lower = lower + image[m][0] * with_image[0] + image[m][1] * with_image[1]
        lower = lower + 1e-06
        active = jnp.where(counts > float(step), 1.0, 0.0)
        alpha = (active * upper[0] / lower, active * upper[1] / lower)
        for m in range(step + 1):
            correction[m] = add(correction[m], mul(alpha, residual[m]))
        residual = residual + [(zero, zero)]
        for m in range(step + 2):
            change = mul(alpha, image[m])
            residual[m] = (residual[m][0] - change[0], residual[m][1] - change[1])
    return correction, residual


def combine(coefs, vectors, sign):
    straight = coefs[0][0] * vectors[0]
    turned = coefs[0][1] * vectors[0]
    for (real, imag), vector in zip(coefs[1:], vectors[1:]):
        straight = straight + real * vector
        turned = turned + imag * vector
    return straight + sign * pltpu.roll(turned, 4, 0)


def update_kernel(sweep, gram_ref, fields_ref, basis_ref, friction_ref, slots_ref, *outs):
    correction, residual = step_sizes(gram_ref, slots_ref, sweep)
    sign = jnp.where(iota((8, LANES), 0) < 4, -1.0, 1.0)

    def update(g, _):
        for comp in range(3):
            vectors = [basis_ref[m, g, comp] for m in range(COUNT)]
            fields = fields_ref[g, comp] + combine(correction, vectors[:LMAX], sign)
            left = combine(residual, vectors, sign)
            if sweep == SWEEPS - 1:
                outs[0][g, comp] = fields
                outs[0][g, 3 + comp] = left
            else:
                outs[0][g, comp] = fields
                outs[1][g, comp] = left if comp == 0 else left + friction_ref[g, comp - 1]
        return 0

    lax.fori_loop(0, RANKS, update, 0)


def struct(*shape):
    return jax.ShapeDtypeStruct(shape, jnp.float32)


def call(kernel, out, specs, scratch=(), mebibytes=16, out_specs=None):
    outs = out if isinstance(out, list) else [out]
    result = pl.pallas_call(
        kernel,
        out_shape=outs,
        in_specs=specs,
        out_specs=out_specs or [VMEM] * len(outs),
        scratch_shapes=list(scratch),
        compiler_params=pltpu.CompilerParams(vmem_limit_bytes=mebibytes * 1024 * 1024),
    )
    return (lambda *args: result(*args)) if isinstance(out, list) else (lambda *args: result(*args)[0])


def exchange(values, axis):
    return lax.all_to_all(values, axis, split_axis=0, concat_axis=0, tiled=True)


def rows_of(x):
    return x.transpose(0, 2, 1, 3).reshape(4, 3, 2, RANKS, LANES).transpose(0, 1, 3, 2, 4).reshape(-1, LANES)


def fields_of(rows):
    return rows.reshape(4, 3, RANKS, 2, LANES).transpose(0, 3, 1, 2, 4).reshape(4, 2, 3, RANKS * LANES)


def body(
    harmonics, forcing, depths, damping, weights, couple_east, couple_north, connections, counts, harmonic_of_slot
):
    whole = pltpu.VMEM((384, LANES), jnp.float32)
    four = pltpu.VMEM((4, 2048), jnp.float32)
    line = pltpu.VMEM((1, 2048), jnp.float32)
    packed = call(
        pack_kernel,
        struct(RANKS, 7, 8, LANES),
        [HBM] * 8,
        (
            whole,
            whole,
            four,
            four,
            four,
            line,
            line,
            pltpu.VMEM((4, RANKS), jnp.int32),
            pltpu.VMEM((RANKS, 1, 2048), jnp.float32),
            pltpu.VMEM((RANKS, 7, 8, LANES), jnp.float32),
            pltpu.SemaphoreType.DMA((8,)),
            pltpu.SemaphoreType.DMA((3,)),
        ),
        58,
        [HBM],
    )(
        rows_of(harmonics),
        rows_of(forcing),
        weights,
        couple_east,
        couple_north,
        damping.reshape(1, -1),
        depths.reshape(1, -1),
        connections.T,
    )
    given = exchange(packed, "node")
    slots = jnp.broadcast_to(harmonic_of_slot.reshape(RANKS, 1, 4), (RANKS, 2, 4)).reshape(1, LANES)
    cosines = np.cos(np.arange(SAMPLES) * (2.0 * math.pi / SAMPLES)).astype(np.float32).reshape(1, SAMPLES)

    synthesis, analysis = call(tables_kernel, [struct(SAMPLES, LANES), struct(LANES, SAMPLES)], [VMEM] * 2)(
        slots, cosines
    )
    table = exchange(call(forward_kernel, struct(RANKS, 5, 8, LANES), [VMEM, HBM])(given, analysis), "freq")

    def friction_of(received):
        terms = call(friction_kernel, struct(RANKS, 2, 8, LANES), [VMEM] * 4)(received, table, synthesis, analysis)
        return exchange(terms, "freq")

    base, links, index, per_slot = call(
        start_kernel,
        [
            struct(RANKS, 3, 8, LANES),
            struct(RANKS, 16, 8, LANES),
            jax.ShapeDtypeStruct((RANKS, 2, 8, LANES), jnp.int32),
            struct(2 + SWEEPS, 8, LANES),
        ],
        [VMEM, VMEM, SMEM, SMEM],
    )(given, table, harmonic_of_slot, counts)
    fields = given
    friction = friction_of(table)
    for sweep in range(SWEEPS):
        basis, gram = call(
            basis_kernel,
            [struct(COUNT, RANKS, 3, 8, LANES), struct(RANKS, 2, LANES)],
            [VMEM] * 4,
            (pltpu.VMEM((LMAX, RANKS, 3, 32, LANES), jnp.float32),),
        )(base, friction, links, index)
        gram = exchange(gram, "node")
        if sweep < SWEEPS - 1:
            outs = [struct(RANKS, 3, 8, LANES), struct(RANKS, 3, 8, LANES)]
        else:
            outs = [struct(RANKS, 6, 8, LANES)]
        results = call(functools.partial(update_kernel, sweep), outs, [VMEM] * 5)(
            gram, fields, basis, friction, per_slot
        )
        if sweep < SWEEPS - 1:
            fields, base = results
            friction = friction_of(exchange(fields, "freq"))
    out = [struct(384, LANES)] * 2
    fields, residual = call(
        unpack_kernel, out, [VMEM], (whole, whole, pltpu.SemaphoreType.DMA((2,))), 16, [HBM] * 2
    )(exchange(results[0], "node"))
    return (fields_of(fields), fields_of(residual))


def solution(mesh):
    return jax.shard_map(
        body,
        mesh=mesh,
        in_specs=(
            P("freq", None, None, "node"),
            P("freq", None, None, "node"),
            P("node"),
            P("node"),
            P(None, "node"),
            P(None, "node"),
            P(None, "node"),
            P("node", None),
            P(),
            P(),
        ),
        out_specs=(P("freq", None, None, "node"), P("freq", None, None, "node")),
        check_vma=False,
    )
```

```python
import functools
import math

import jax
import jax.numpy as jnp
import numpy as np
from jax import lax
from jax.experimental import pallas as pl
from jax.experimental.pallas import tpu as pltpu
from jax.sharding import PartitionSpec as P

SAMPLES = 128
LMAX = 5
SWEEPS = 2

FRICTION = 2.0
CORIOLIS = 0.5
ETA_DAMP = 0.2
OMEGA_STEP = 0.05
SPEED_FLOOR = 0.01
TOP_HARMONIC = lax.Precision.HIGHEST

RANKS = 16
LANES = 128
SHARE = 8
COUNT = LMAX + 1
REAL_PAIRS = [(m, n) for m in range(COUNT) for n in range(m, COUNT)]
IMAG_PAIRS = [(m, n) for m in range(COUNT) for n in range(m + 1, COUNT)]
ROW_DAMPING, ROW_DEPTHS, ROW_LINKS = 12, 13, 14

VMEM = pl.BlockSpec(memory_space=pltpu.VMEM)
HBM = pl.BlockSpec(memory_space=pl.ANY)
SMEM = pl.BlockSpec(memory_space=pltpu.SMEM)


def iota(shape, axis):
    return lax.broadcasted_iota(jnp.int32, shape, axis)


def swap_blocks(rows):
    lane = iota((8, LANES), 1)
    rows = list(rows)
    for bit in range(4):
        step = SHARE << bit
        upper = (lane & step) != 0
        for i in range(RANKS):
            if i & (1 << bit):
                continue
            low, high = rows[i], rows[i | (1 << bit)]
            crossing = jnp.where(upper, low, high)
            crossed = jnp.take_along_axis(crossing, lane ^ step, axis=1, mode="promise_in_bounds")
            rows[i] = jnp.where(upper, crossed, low)
            rows[i | (1 << bit)] = jnp.where(upper, high, crossed)
    return rows


def pack_group(rows_of, out_ref, group):
    rows = [rows_of(b) for b in range(RANKS)]
    for rank, row in enumerate(swap_blocks(rows)):
        out_ref[rank, group] = row


def pack_kernel(
    fields_hbm,
    forcing_hbm,
    weights_hbm,
    east_hbm,
    north_hbm,
    damping_hbm,
    depths_hbm,
    links_hbm,
    out_hbm,
    fields_ref,
    forcing_ref,
    weights_ref,
    east_ref,
    north_ref,
    damping_ref,
    depths_ref,
    links_ref,
    rows_ref,
    out_ref,
    sems,
    out_sems,
):
    sources = (fields_hbm, forcing_hbm, weights_hbm, east_hbm, north_hbm, damping_hbm, depths_hbm, links_hbm)
    targets = (fields_ref, forcing_ref, weights_ref, east_ref, north_ref, damping_ref, depths_ref, links_ref)
    copies = [pltpu.make_async_copy(a, b, sems.at[i]) for i, (a, b) in enumerate(zip(sources, targets))]
    for copy in copies:
        copy.start()
    sent = []

    def send(index, group, count):
        part = pl.ds(group, count)
        copy = pltpu.make_async_copy(out_ref.at[:, part], out_hbm.at[:, part], out_sems.at[index])
        copy.start()
        sent.append(copy)

    for group in range(6):
        if group % 3 == 0:
            copies[group // 3].wait()
        source = (fields_ref, forcing_ref)[group // 3]

        def block(b):
            start = 32 * (group % 3) + 2 * b
            parts = [source[pl.ds(start + part, 4, stride=96), :] for part in range(2)]
            return jnp.concatenate(parts, axis=0)

        pack_group(block, out_ref, group)
        if group % 3 == 2:
            send(group // 3, group - 2, 3)
    for copy in copies[2:]:
        copy.wait()
    for kind, source in enumerate((weights_ref, east_ref, north_ref)):
        for link in range(4):
            rows_ref[4 * kind + link] = source[link : link + 1, :]
    rows_ref[ROW_DAMPING] = damping_ref[...]
    rows_ref[ROW_DEPTHS] = depths_ref[...]
    local = (links_ref[...] - lax.axis_index("node") * RANKS).astype(jnp.float32)
    for link in range(2):
        for b in range(RANKS):
            row = jnp.broadcast_to(local[2 + link : 3 + link, b : b + 1], (1, LANES))
            rows_ref[ROW_LINKS + link, :, LANES * b : LANES * (b + 1)] = row
    mine = lax.axis_index("freq")
    rows = [jnp.broadcast_to(rows_ref[mine, :, LANES * b : LANES * (b + 1)], (8, LANES)) for b in range(RANKS)]
    diagonal = jnp.sum(weights_ref[...], axis=0, keepdims=True) + (2.0 / 3.0) * damping_ref[...] + ETA_DAMP / 3.0
    mean = jnp.sum(diagonal, axis=1, keepdims=True) * (1.0 / diagonal.shape[1])
    top = iota((8, LANES), 0) == 0
    for rank, row in enumerate(swap_blocks(rows)):
        out_ref[rank, 6] = jnp.where(top, row, mean)
    send(2, 6, 1)
    for copy in sent:
        copy.wait()


def forward_kernel(given_ref, _, out_ref):
    for half in range(2):
        rows = jnp.concatenate([given_ref[8 * half + i, 6, 0:1] for i in range(8)], axis=0)
        for rank in range(RANKS):
            out_ref[rank, 3 + half] = rows
    for rank in range(RANKS):
        for comp in range(3):
            out_ref[rank, comp] = given_ref[rank, comp]


def unpack_kernel(x_ref, fields_hbm, residual_hbm, fields_ref, residual_ref, sems):
    copies = []
    for i, (target, out) in enumerate(((fields_ref, fields_hbm), (residual_ref, residual_hbm))):
        for comp in range(3):
            rows = swap_blocks([x_ref[rank, 3 * i + comp] for rank in range(RANKS)])
            for b, row in enumerate(rows):
                for part in range(2):
                    target[pl.ds(32 * comp + 2 * b + part, 4, stride=96), :] = row[4 * part : 4 * part + 4]
        copies.append(pltpu.make_async_copy(target, out, sems.at[i]))
        copies[-1].start()
    for copy in copies:
        copy.wait()


def tables_kernel(harmonic_ref, cosines_ref, synthesis_ref, analysis_ref):
    samples = iota((SAMPLES, LANES), 0)
    quarter = jnp.where((iota((SAMPLES, LANES), 1) & 4) != 0, SAMPLES // 4, 0)
    harmonic = jnp.broadcast_to(harmonic_ref[...], (SAMPLES, LANES))
    turn = (samples * harmonic + quarter) & (SAMPLES - 1)
    cosines = jnp.broadcast_to(cosines_ref[...], (SAMPLES, LANES))
    synthesis = jnp.take_along_axis(cosines, turn, axis=1, mode="promise_in_bounds")
    synthesis_ref[...] = synthesis
    analysis_ref[...] = (synthesis * jnp.where(harmonic == 0, 1.0 / SAMPLES, 2.0 / SAMPLES)).T


def friction_kernel(x_ref, table_ref, synthesis_ref, analysis_ref, out_ref):
    moments = [
        jnp.dot(
            synthesis_ref[...],
            x_ref[:, comp].reshape(LANES, LANES),
            precision=TOP_HARMONIC,
            preferred_element_type=jnp.float32,
        )
        for comp in range(3)
    ]
    elevation, eastward, northward = moments
    group = lax.axis_index("freq")
    depths = table_ref[ROW_DEPTHS, 3 + group // 8]
    depth = jnp.sum(jnp.where(iota((8, LANES), 0) == group % 8, depths, 0.0), axis=0, keepdims=True)
    column_depth = depth + 0.5 * jnp.tanh(elevation)
    magnitude = jnp.sqrt(eastward * eastward + northward * northward + SPEED_FLOOR)
    factor = FRICTION * magnitude / column_depth
    for comp, moving in enumerate((eastward, northward)):
        terms = jnp.dot(
            analysis_ref[...], factor * moving, precision=TOP_HARMONIC, preferred_element_type=jnp.float32
        )
        out_ref[:, comp] = terms.reshape(RANKS, 8, LANES)


def prepare_links(table_ref, shift, links_ref, index_ref):
    share = iota((8, LANES), 1) & (SHARE - 1)
    for half in range(2):
        rows = [table_ref[at, 3 + half] for at in range(RANKS)]
        spread = rows[0] + rows[1] + rows[2] + rows[3]
        values = rows[:12] + [
            spread + (ETA_DAMP - shift),
            spread + (rows[ROW_DAMPING] - shift),
            rows[4] + rows[5] + rows[6] + rows[7],
            rows[8] + rows[9] + rows[10] + rows[11],
        ]
        for i in range(8):
            for at, value in enumerate(values):
                links_ref[8 * half + i, at] = jnp.broadcast_to(value[i : i + 1], (8, LANES))
        for link in range(2):
            at = rows[ROW_LINKS + link].astype(jnp.int32)
            outside = jnp.logical_or(at < 0, at > RANKS - 1)
            lane = (at & (RANKS - 1)) * SHARE + share
            index = jnp.where(outside, lane + LANES, lane)
            for i in range(8):
                index_ref[8 * half + i, link] = jnp.broadcast_to(index[i : i + 1], (8, LANES))


def apply_operator(vectors, links_ref, index_ref):
    lane = iota((8, LANES), 1)
    first = lane < SHARE
    last = lane >= LANES - SHARE
    result = []
    for g in range(RANKS):
        here = vectors[g]
        before = vectors[g - 1] if g > 0 else [pltpu.roll(x, LANES - 2 * SHARE, 1) for x in here]
        after = vectors[g + 1] if g < RANKS - 1 else [pltpu.roll(x, 2 * SHARE, 1) for x in here]
        beside = []
        beside.append([pltpu.roll(jnp.where(last, p, x), SHARE, 1) for p, x in zip(before, here)])
        beside.append([pltpu.roll(jnp.where(first, n, x), LANES - SHARE, 1) for n, x in zip(after, here)])
        edges = [jnp.where(last, p, n) for p, n in zip(before, after)]
        for link in range(2):
            index = index_ref[g, link]
            outside = index >= LANES
            index = index & (LANES - 1)
            beside.append(
                [
                    jnp.where(
                        outside,
                        jnp.take_along_axis(e, index, axis=1, mode="promise_in_bounds"),
                        jnp.take_along_axis(x, index, axis=1, mode="promise_in_bounds"),
                    )
                    for e, x in zip(edges, here)
                ]
            )
        x_ele, x_east, x_north = here
        eta_sum, flow_sum, east_sum, north_sum = [links_ref[g, 12 + at] for at in range(4)]
        ele = eta_sum * x_ele - east_sum * x_east - north_sum * x_north
        east = flow_sum * x_east - east_sum * x_ele - CORIOLIS * x_north
        north = flow_sum * x_north - north_sum * x_ele + CORIOLIS * x_east
        for link in range(4):
            y_ele, y_east, y_north = beside[link]
            weight, to_east, to_north = [links_ref[g, at + link] for at in (0, 4, 8)]
            ele = ele - weight * y_ele + to_east * y_east + to_north * y_north
            east = east - weight * y_east + to_east * y_ele
            north = north - weight * y_north + to_north * y_ele
        result.append([ele, east, north])
    return result


def slot_rows(ref, pick):
    first = lax.axis_index("freq") * 4
    slot = iota((8, LANES), 0) & 3
    values = [pick(ref, first + s) for s in range(4)]
    return jnp.where(slot == 0, values[0], jnp.where(slot == 1, values[1], jnp.where(slot == 2, values[2], values[3])))


def angular_rows(harmonic_ref):
    return OMEGA_STEP * slot_rows(harmonic_ref, lambda ref, i: ref[i]).astype(jnp.float32)


def start_kernel(given_ref, table_ref, harmonic_ref, counts_ref, _, base_ref, links_ref, index_ref, slots_ref):
    shift = given_ref[0, 6, 1:2]
    for g in range(1, RANKS):
        shift = shift + given_ref[g, 6, 1:2]
    shift = jnp.broadcast_to(shift * (1.0 / RANKS), (8, LANES))
    angular = angular_rows(harmonic_ref)
    slots_ref[0] = shift
    slots_ref[1] = angular
    for sweep in range(SWEEPS):
        slots_ref[2 + sweep] = slot_rows(counts_ref, lambda ref, i: ref[sweep, i]).astype(jnp.float32)
    prepare_links(table_ref, shift, links_ref, index_ref)
    turn = angular * jnp.where(iota((8, LANES), 0) < 4, -1.0, 1.0)
    vectors = [[given_ref[g, comp] for comp in range(3)] for g in range(RANKS)]
    images = apply_operator(vectors, links_ref, index_ref)
    for g in range(RANKS):
        for comp in range(3):
            rest = shift * vectors[g][comp] + turn * pltpu.roll(vectors[g][comp], 4, 0)
            base_ref[g, comp] = given_ref[g, 3 + comp] - images[g][comp] - rest


def basis_kernel(base_ref, friction_ref, links_ref, index_ref, basis_ref, gram_ref, swap_ref):
    for g in range(RANKS):
        basis_ref[0, g, 0] = base_ref[g, 0]
        basis_ref[0, g, 1] = base_ref[g, 1] - friction_ref[g, 0]
        basis_ref[0, g, 2] = base_ref[g, 2] - friction_ref[g, 1]

    def power(m, _):
        vectors = [[basis_ref[m, g, comp] for comp in range(3)] for g in range(RANKS)]
        images = apply_operator(vectors, links_ref, index_ref)
        for g in range(RANKS):
            for comp in range(3):
                basis_ref[m + 1, g, comp] = images[g][comp]
                swap_ref[m, g, comp, pl.ds(0, 8, stride=2), :] = images[g][comp]
                swap_ref[m, g, comp, pl.ds(16, 8, stride=2), :] = images[g][comp]
        return 0

    lax.fori_loop(0, LMAX, power, 0)

    def products(g, sums):
        for comp in range(3):
            vectors = [basis_ref[m, g, comp] for m in range(COUNT)]
            turned = [None] + [swap_ref[m, g, comp, pl.ds(8, 8, stride=2), :] for m in range(LMAX)]
            terms = [vectors[m] * vectors[n] for m, n in REAL_PAIRS]
            terms += [vectors[m] * turned[n] for m, n in IMAG_PAIRS]
            sums = tuple(a + b for a, b in zip(sums, terms))
        return sums

    entries = len(REAL_PAIRS) + len(IMAG_PAIRS)
    sums = lax.fori_loop(0, RANKS, products, tuple(jnp.zeros((8, LANES), jnp.float32) for _ in range(entries)))
    lane = iota((8, LANES), 1)
    gram = jnp.zeros((8, LANES), jnp.float32)
    for entry, value in enumerate(sums):
        gram = jnp.where(lane == entry, jnp.sum(value, axis=1, keepdims=True), gram)
    turned = pltpu.roll(gram, 4, 0)
    gram = jnp.where(lane < len(REAL_PAIRS), gram + turned, gram - turned)
    packed = jnp.where(lane < LANES // 2, gram, pltpu.roll(pltpu.roll(gram, LANES // 2, 1), 6, 0))[:2]
    for rank in range(RANKS):
        gram_ref[rank] = packed


def step_sizes(gram_ref, slots_ref, sweep):
    gram = gram_ref[0]
    for rank in range(1, RANKS):
        gram = gram + gram_ref[rank]
    swapped = pltpu.roll(gram, LANES // 2, 1)
    gram = jnp.concatenate([gram, swapped, gram, swapped], axis=0)

    def entry(values, at):
        return jnp.broadcast_to(values[:, at : at + 1], (8, LANES))

    inner = {}
    for at, (m, n) in enumerate(REAL_PAIRS):
        inner[m, n] = (entry(gram, at), None)
    for at, (m, n) in enumerate(IMAG_PAIRS):
        inner[m, n] = (inner[m, n][0], entry(gram, len(REAL_PAIRS) + at))

    def mul(a, b):
        return (a[0] * b[0] - a[1] * b[1], a[0] * b[1] + a[1] * b[0])

    def add(a, b):
        return (a[0] + b[0], a[1] + b[1])

    def conj_mul(a, b):
        return (a[0] * b[0] + a[1] * b[1], a[0] * b[1] - a[1] * b[0])

    def gram_times(m, n, b):
        if m == n:
            g = inner[m, n][0]
            return (g * b[0], g * b[1])
        if m < n:
            return mul(inner[m, n], b)
        return conj_mul(inner[n, m], b)

    shift, angular, counts = slots_ref[0], slots_ref[1], slots_ref[2 + sweep]
    zero = jnp.zeros((8, LANES), jnp.float32)
    residual = [(jnp.ones((8, LANES), jnp.float32), zero)]
    correction = [(zero, zero) for _ in range(LMAX)]
    for step in range(LMAX):
        image = []
        for m in range(step + 2):
            value = (zero, zero)
            if m <= step:
                r = residual[m]
                value = (shift * r[0] - angular * r[1], shift * r[1] + angular * r[0])
            if m > 0:
                value = add(value, residual[m - 1])
            image.append(value)
        upper = (zero, zero)
        lower = zero
        for m in range(step + 2):
            with_residual = (zero, zero)
            for n in range(step + 1):
                with_residual = add(with_residual, gram_times(m, n, residual[n]))
            upper = add(upper, conj_mul(image[m], with_residual))
            with_image = (zero, zero)
            for n in range(step + 2):
                with_image = add(with_image, gram_times(m, n, image[n]))
            lower = lower + image[m][0] * with_image[0] + image[m][1] * with_image[1]
        lower = lower + 1e-06
        active = jnp.where(counts > float(step), 1.0, 0.0)
        alpha = (active * upper[0] / lower, active * upper[1] / lower)
        for m in range(step + 1):
            correction[m] = add(correction[m], mul(alpha, residual[m]))
        residual = residual + [(zero, zero)]
        for m in range(step + 2):
            change = mul(alpha, image[m])
            residual[m] = (residual[m][0] - change[0], residual[m][1] - change[1])
    return correction, residual


def combine(coefs, vectors, sign):
    straight = coefs[0][0] * vectors[0]
    turned = coefs[0][1] * vectors[0]
    for (real, imag), vector in zip(coefs[1:], vectors[1:]):
        straight = straight + real * vector
        turned = turned + imag * vector
    return straight + sign * pltpu.roll(turned, 4, 0)


def update_kernel(sweep, gram_ref, fields_ref, basis_ref, friction_ref, slots_ref, *outs):
    correction, residual = step_sizes(gram_ref, slots_ref, sweep)
    sign = jnp.where(iota((8, LANES), 0) < 4, -1.0, 1.0)

    def update(g, _):
        for comp in range(3):
            vectors = [basis_ref[m, g, comp] for m in range(COUNT)]
            fields = fields_ref[g, comp] + combine(correction, vectors[:LMAX], sign)
            left = combine(residual, vectors, sign)
            if sweep == SWEEPS - 1:
                outs[0][g, comp] = fields
                outs[0][g, 3 + comp] = left
            else:
                outs[0][g, comp] = fields
                outs[1][g, comp] = left if comp == 0 else left + friction_ref[g, comp - 1]
        return 0

    lax.fori_loop(0, RANKS, update, 0)


def struct(*shape):
    return jax.ShapeDtypeStruct(shape, jnp.float32)


def call(kernel, out, specs, scratch=(), mebibytes=16, out_specs=None):
    outs = out if isinstance(out, list) else [out]
    result = pl.pallas_call(
        kernel,
        out_shape=outs,
        in_specs=specs,
        out_specs=out_specs or [VMEM] * len(outs),
        scratch_shapes=list(scratch),
        compiler_params=pltpu.CompilerParams(vmem_limit_bytes=mebibytes * 1024 * 1024),
    )
    return (lambda *args: result(*args)) if isinstance(out, list) else (lambda *args: result(*args)[0])


def exchange(values, axis):
    return lax.all_to_all(values, axis, split_axis=0, concat_axis=0, tiled=True)


def rows_of(x):
    return x.transpose(0, 2, 1, 3).reshape(4, 3, 2, RANKS, LANES).transpose(0, 1, 3, 2, 4).reshape(-1, LANES)


def fields_of(rows):
    return rows.reshape(4, 3, RANKS, 2, LANES).transpose(0, 3, 1, 2, 4).reshape(4, 2, 3, RANKS * LANES)


def body(
    harmonics, forcing, depths, damping, weights, couple_east, couple_north, connections, counts, harmonic_of_slot
):
    whole = pltpu.VMEM((384, LANES), jnp.float32)
    four = pltpu.VMEM((4, 2048), jnp.float32)
    line = pltpu.VMEM((1, 2048), jnp.float32)
    packed = call(
        pack_kernel,
        struct(RANKS, 7, 8, LANES),
        [HBM] * 8,
        (
            whole,
            whole,
            four,
            four,
            four,
            line,
            line,
            pltpu.VMEM((4, RANKS), jnp.int32),
            pltpu.VMEM((RANKS, 1, 2048), jnp.float32),
            pltpu.VMEM((RANKS, 7, 8, LANES), jnp.float32),
            pltpu.SemaphoreType.DMA((8,)),
            pltpu.SemaphoreType.DMA((3,)),
        ),
        58,
        [HBM],
    )(
        rows_of(harmonics),
        rows_of(forcing),
        weights,
        couple_east,
        couple_north,
        damping.reshape(1, -1),
        depths.reshape(1, -1),
        connections.T,
    )
    given = exchange(packed, "node")
    slots = jnp.broadcast_to(harmonic_of_slot.reshape(RANKS, 1, 4), (RANKS, 2, 4)).reshape(1, LANES)
    cosines = np.cos(np.arange(SAMPLES) * (2.0 * math.pi / SAMPLES)).astype(np.float32).reshape(1, SAMPLES)

    synthesis, analysis = call(tables_kernel, [struct(SAMPLES, LANES), struct(LANES, SAMPLES)], [VMEM] * 2)(
        slots, cosines
    )
    table = exchange(call(forward_kernel, struct(RANKS, 5, 8, LANES), [VMEM, HBM])(given, analysis), "freq")

    def friction_of(received):
        terms = call(friction_kernel, struct(RANKS, 2, 8, LANES), [VMEM] * 4)(received, table, synthesis, analysis)
        return exchange(terms, "freq")

    friction = friction_of(table)
    base, links, index, per_slot = call(
        start_kernel,
        [
            struct(RANKS, 3, 8, LANES),
            struct(RANKS, 16, 8, LANES),
            jax.ShapeDtypeStruct((RANKS, 2, 8, LANES), jnp.int32),
            struct(2 + SWEEPS, 8, LANES),
        ],
        [VMEM, VMEM, SMEM, SMEM, VMEM],
    )(given, table, harmonic_of_slot, counts, friction)
    fields = given
    for sweep in range(SWEEPS):
        basis, gram = call(
            basis_kernel,
            [struct(COUNT, RANKS, 3, 8, LANES), struct(RANKS, 2, LANES)],
            [VMEM] * 4,
            (pltpu.VMEM((LMAX, RANKS, 3, 32, LANES), jnp.float32),),
        )(base, friction, links, index)
        gram = exchange(gram, "node")
        if sweep < SWEEPS - 1:
            outs = [struct(RANKS, 3, 8, LANES), struct(RANKS, 3, 8, LANES)]
        else:
            outs = [struct(RANKS, 6, 8, LANES)]
        results = call(functools.partial(update_kernel, sweep), outs, [VMEM] * 5)(
            gram, fields, basis, friction, per_slot
        )
        if sweep < SWEEPS - 1:
            fields, base = results
            friction = friction_of(exchange(fields, "freq"))
    out = [struct(384, LANES)] * 2
    fields, residual = call(
        unpack_kernel, out, [VMEM], (whole, whole, pltpu.SemaphoreType.DMA((2,))), 16, [HBM] * 2
    )(exchange(results[0], "node"))
    return (fields_of(fields), fields_of(residual))


def solution(mesh):
    return jax.shard_map(
        body,
        mesh=mesh,
        in_specs=(
            P("freq", None, None, "node"),
            P("freq", None, None, "node"),
            P("node"),
            P("node"),
            P(None, "node"),
            P(None, "node"),
            P(None, "node"),
            P("node", None),
            P(),
            P(),
        ),
        out_specs=(P("freq", None, None, "node"), P("freq", None, None, "node")),
        check_vma=False,
    )
```
